32 devices in a mesh: sx: 2 (over x), sy: 4 (over y, core), ta: 4 (over z).
Axes of the slice: x: 2, y: 2, z: 4, core: 2. Of those that a mesh axis runs over, the one named last changes fastest.
Arguments:
- velocity: bfloat16 [3, 256, 8, 1024], P(None, 'ta', 'sx', 'sy'), may hold values from -6 to 6
- seeds_first: int32 [64, 64], replicated, may hold values from -64 to 64
- seeds_merge: int32 [2, 128, 64], replicated, may hold values from -64 to 64
Outputs:
- basis: float32 [64, 5, 8, 1024], P(None, None, 'sx', ('sy', 'ta'))
The draws below stay inside these ranges and needn't reach their ends.
All inputs are finite; a program needn't handle non-finite values.
Results may differ from the reference program's by a relative error of at most 0.0008.
Values may be sent and summed in bfloat16 or wider, within the bound.
A program may use at most 64 MiB of HBM per device.

```python
import jax
import jax.numpy as jnp
from jax import lax

RANK = 64
LEVELS = 2
NX = 8
NY = 1024
SNAPS = 256
N_TA = 4


def touch_ends(entries, own_key, low, largest):
    extent = entries.shape
    place = [jax.random.randint(jax.random.fold_in(own_key, axis), (), 0, extent[axis]) for axis in range(len(extent))]
    entries = entries.at[tuple(place)].set(low)
    longest = extent.index(max(extent))
    place[longest] = (place[longest] + 1) % extent[longest]
    return entries.at[tuple(place)].set(largest)


def levels(key, shape, split, smallest, largest):
    loudness, own = 1.0, jax.random.fold_in(key, 6)
    for dim, blocks in split:
        draws = jnp.exp(jax.random.uniform(jax.random.fold_in(own, dim), (blocks,), jnp.float32, smallest / len(split), largest / len(split)))
        loudness = loudness * jnp.repeat(draws, shape[dim] // blocks).reshape([-1 if axis == dim else 1 for axis in range(len(shape))])
    return loudness


def noise(stream_key, dims, spread, bound, split=(), kind=jnp.bfloat16):
    gain = levels(stream_key, dims, split, -0.22, 0.18) if split else 1.0
    result = jax.random.normal(stream_key, dims, jnp.float32) * spread * gain
    return jnp.minimum(jnp.maximum(result, -bound), bound).astype(kind)


def setup_inputs(seed: int = 0) -> dict:
    streams_of = jax.random.split(jax.random.key(seed), 4)
    return {
        "velocity": noise(streams_of[0], (3, SNAPS, NX, NY), 1.0, 6.0, ((1, 4), (2, 2), (3, 4))),
        "seeds_first": touch_ends(jax.random.randint(streams_of[1], (RANK, RANK), -64, 65), jax.random.fold_in(streams_of[1], 1), -64, 64).astype(jnp.int32),
        "seeds_merge": touch_ends(jax.random.randint(streams_of[2], (LEVELS, 2 * RANK, RANK), -64, 65), jax.random.fold_in(streams_of[2], 1), -64, 64).astype(jnp.int32),
    }


def matmul_hi(left, right):
    return jnp.dot(left, right, precision=lax.Precision.HIGHEST)

def coefficients(gram_mat, rotation):
    order_n = gram_mat.shape[0]
    scaling = jnp.sqrt(jnp.trace(gram_mat) / order_n)
    imaged = matmul_hi(gram_mat, rotation)
    reduced = matmul_hi(rotation.T, imaged)
    factor = jnp.linalg.cholesky(reduced)
    solved = jax.scipy.linalg.solve_triangular(factor, imaged.T, lower=True)
    return solved.T / scaling

def diff_x(field):
    return 0.5 * (field[:, 2:, 1:-1] - field[:, :-2, 1:-1])

def diff_y(field):
    return 0.5 * (field[:, 1:-1, 2:] - field[:, 1:-1, :-2])

def strain_rows(padded):
    comp_u = padded[0]
    comp_v = padded[1]
    comp_w = padded[2]
    fields = jnp.stack([diff_x(comp_u), diff_y(comp_v), 0.5 * (diff_y(comp_u) + diff_x(comp_v)), 0.5 * diff_x(comp_w), 0.5 * diff_y(comp_w)], axis=1)
    return fields.reshape(fields.shape[0], -1)

def rotations(seeds_first, seeds_merge):
    width = seeds_first.shape[0]
    first = jnp.eye(width, dtype=jnp.float32) + seeds_first.astype(jnp.float32) * (0.5 / (64.0 * 8.0))
    stacked = jnp.concatenate([jnp.eye(width, dtype=jnp.float32), jnp.eye(width, dtype=jnp.float32)], axis=0) / jnp.sqrt(jnp.float32(2.0))
    merges = stacked[None] + seeds_merge.astype(jnp.float32) * (0.5 / (64.0 * jnp.sqrt(jnp.float32(128.0))))
    return (first, merges)

def reference(velocity, seeds_first, seeds_merge):
    rotation_first, rotation_merge = rotations(seeds_first, seeds_merge)
    bases = []
    for blk_idx in range(N_TA):
        snap_block = velocity[:, blk_idx * RANK:(blk_idx + 1) * RANK].astype(jnp.float32)
        padded = jnp.pad(snap_block, ((0, 0), (0, 0), (1, 1), (1, 1)))
        strain = strain_rows(padded)
        gram_mat = matmul_hi(strain, strain.T)
        kmat = coefficients(gram_mat, rotation_first)
        bases.append(matmul_hi(kmat.T, strain))
    for depth_at in range(LEVELS):
        merged = []
        for pair_idx in range(len(bases) // 2):
            stacked = jnp.concatenate([bases[2 * pair_idx], bases[2 * pair_idx + 1]], axis=0)
            gram_mat = matmul_hi(stacked, stacked.T)
            kmat = coefficients(gram_mat, rotation_merge[depth_at])
            merged.append(matmul_hi(kmat.T, stacked))
        bases = merged
    return bases[0].reshape(RANK, 5, NX, NY)
```

```python
import functools

import jax
import jax.numpy as jnp
from jax import lax
from jax.experimental import pallas as pl
from jax.experimental.pallas import tpu as pltpu
from jax.sharding import PartitionSpec as P

HI = lax.Precision.HIGHEST
MESH = pl.DeviceIdType.MESH
OWNERS = 16


def mm(left, right, contract=(1, 0)):
    return lax.dot_general(
        left,
        right,
        (((contract[0],), (contract[1],)), ((), ())),
        precision=HI,
        preferred_element_type=jnp.float32,
    )


def dot16(left, right, contract=(1, 0)):
    return lax.dot_general(
        left,
        right,
        (((contract[0],), (contract[1],)), ((), ())),
        preferred_element_type=jnp.float32,
    )


def iotas(rows, cols):
    return (
        lax.broadcasted_iota(jnp.int32, (rows, cols), 0),
        lax.broadcasted_iota(jnp.int32, (rows, cols), 1),
    )


def eye(rows, cols):
    row, col = iotas(rows, cols)
    return (row == col).astype(jnp.float32)


def signed_half(plus, minus):
    return (0.5 * plus.astype(jnp.float32) - 0.5 * minus.astype(jnp.float32)).astype(jnp.bfloat16)


def eliminate(mats, sides):
    n = mats[0].shape[0]
    batch = len(mats)
    tiles = n // 8
    width = 2 * n
    work = [
        [jnp.concatenate([m, s], axis=1)[8 * i : 8 * i + 8] for i in range(tiles)]
        for m, s in zip(mats, sides)
    ]
    sub = lax.broadcasted_iota(jnp.int32, (8, width), 0)
    done = [[None] * tiles for _ in range(batch)]
    for p in range(tiles):
        cols = [
            [
                [
                    jnp.broadcast_to(work[b][i][:, 8 * p + k : 8 * p + k + 1], (8, width))
                    for i in range(p, tiles)
                ]
                for k in range(8)
            ]
            for b in range(batch)
        ]
        for b in range(batch):
            head = work[b][p]
            rest = [work[b][i] for i in range(p + 1, tiles)]
            scales = jnp.zeros((8, width), jnp.float32)
            for k in range(8):
                pivot = cols[b][k][0][k : k + 1]
                inv = 1.0 / pivot
                scales = jnp.where(sub == k, jnp.broadcast_to(inv, (8, width)), scales)
                row = head[k : k + 1] * inv
                across = [cols[b][j][0][k : k + 1] * inv for j in range(k + 1, 8)]
                below = jnp.where(sub > k, cols[b][k][0], 0.0)
                head = head - below * row
                for j in range(k + 1, 8):
                    cols[b][j][0] = cols[b][j][0] - below * across[j - k - 1]
                for i in range(1, tiles - p):
                    factor = cols[b][k][i]
                    rest[i - 1] = rest[i - 1] - factor * row
                    for j in range(k + 1, 8):
                        cols[b][j][i] = cols[b][j][i] - factor * across[j - k - 1]
            done[b][p] = head * jnp.sqrt(scales)
            for i in range(p + 1, tiles):
                work[b][i] = rest[i - p - 1]
    return [jnp.concatenate(done[b], axis=0)[:, n:] for b in range(batch)]


def total(entries):
    return jnp.sum(jnp.sum(entries, axis=0, keepdims=True), axis=1, keepdims=True)


def first_level(grams, first):
    width = first.shape[0]
    ident = eye(width, width)
    images = [mm(first, g, (0, 0)) for g in grams]
    reduced = [mm(z, first) for z in images]
    solved = eliminate(reduced, images)
    return [c * lax.rsqrt(total(g * ident) / width) for c, g in zip(solved, grams)]


def middle_level(pairs, coefs, turn):
    width = turn.shape[0]
    ident = eye(width, width)
    reduced, sides, scales = [], [], []
    for gram, (low, high) in zip(pairs, coefs):
        lean = jnp.concatenate(
            [mm(low, turn[:, :width], (0, 1)), mm(high, turn[:, width:], (0, 1))], axis=0
        )
        image = mm(lean, gram, (0, 0))
        reduced.append(mm(image, lean))
        norms = [mm(c, c, (0, 0)) for c in (low, high)]
        sides.append(
            jnp.concatenate([mm(image[:, :width], norms[0]), mm(image[:, width:], norms[1])], axis=1)
        )
        trace = total(norms[0] * gram[:width, :width]) + total(norms[1] * gram[width:, width:])
        scales.append(lax.rsqrt(trace / (2 * width)))
    inverses = eliminate(reduced, [ident] * len(pairs))
    return [mm(inv, s) * k for inv, s, k in zip(inverses, sides, scales)]


def last_level(pairs, cross, weights, turn):
    width = turn.shape[0]
    lean = [mm(weights[u], turn[:, u * width : (u + 1) * width], (0, 1)) for u in (0, 1)]
    image = [mm(lean[u], pairs[u], (0, 0)) for u in (0, 1)]
    norms = [mm(weights[u], weights[u], (0, 0)) for u in (0, 1)]
    up = mm(lean[1], cross, (0, 0))
    down = mm(lean[0], cross, (0, 1))
    mixed = mm(up, lean[0])
    reduced = mm(image[0], lean[0]) + mm(image[1], lean[1]) + (mixed + mixed.T)
    trace = total(norms[0] * pairs[0]) + total(norms[1] * pairs[1])
    sides = jnp.concatenate([mm(image[0] + up, norms[0]), mm(image[1] + down, norms[1])], axis=1)
    inverse = eliminate([reduced], [eye(width, width)])[0]
    return mm(inverse, sides) * lax.rsqrt(trace / (2 * width))


def gather_kernel(
    quarter, nx, ny, nt,
    velocity_hbm, first_hbm, merge_hbm,
    coarse_ref, fine_ref, weight_ref,
    velocity, seeds_first, seeds_merge, chunk, edge_low, edge_high, column, rim_out,
    rims, land_pair, land_far, column_pair, column_far, halo,
    side_coarse, side_fine, parts_pair, parts_cross, landed_pair, landed_cross, whole_pair, whole_cross,
    load_sems, chunk_sems, column_sems, rim_sems, low_sems, high_sems,
    scatter_sems, scatter_in, spread_sems, spread_in,
):
    ix, iy, it = lax.axis_index("sx"), lax.axis_index("sy"), lax.axis_index("ta")
    plane = nx * ny
    devices = plane * nt
    place = ix * ny + iy
    me = it * plane + place
    rows3, lanes = chunk.shape[1:]
    snaps = rows3 // 3
    cells_x = lanes // quarter
    half3 = rows3 // 2
    odd, upper = lax.rem(it, 2), lax.div(it, 2)
    partner = it + 1 - 2 * odd
    near, far = lax.rem(it + 2, 4), 3 - it
    b16, f32 = jnp.bfloat16, jnp.float32

    def device(t):
        where = lax.rem(t, plane)
        return (lax.div(where, ny), lax.rem(where, ny), lax.div(t, plane))

    def copy(src, dst, send, recv, target):
        return pltpu.make_async_remote_copy(
            src_ref=src, dst_ref=dst, send_sem=send, recv_sem=recv, device_id=target, device_id_type=MESH
        )

    loads = [
        pltpu.make_async_copy(src, dst, load_sems.at[i])
        for i, (src, dst) in enumerate(
            ((velocity_hbm, velocity), (first_hbm, seeds_first), (merge_hbm, seeds_merge))
        )
    ]
    for c in loads:
        c.start()

    barrier = pltpu.get_barrier_semaphore()

    def greet(target):
        pl.semaphore_signal(barrier, inc=1, device_id=target, device_id_type=MESH)

    def greet_plane(j, carry):
        t = lax.rem(place + j, plane)
        greet((lax.div(t, ny), lax.rem(t, ny), it))
        return carry

    others = (partner, near, far)
    for t in others:
        greet((ix, iy, t))
    can_up, can_down = ix < nx - 1, ix > 0
    for ok, step in ((can_up, 1), (can_down, -1)):
        @pl.when(ok)
        def _():
            for t in others:
                greet((ix + step, iy, t))
    lax.fori_loop(1, plane, greet_plane, 0)
    expected = plane - 1 + 3 + jnp.where(can_up, 3, 0) + jnp.where(can_down, 3, 0)

    right_ok, left_ok = iy + 1 < ny, iy > 0

    @pl.when(jnp.logical_not(can_down))
    def _():
        halo[:, :, :128] = jnp.zeros((6, half3, 128), b16)

    @pl.when(jnp.logical_not(can_up))
    def _():
        halo[:, :, 128:] = jnp.zeros((6, half3, 128), b16)

    @pl.when(jnp.logical_not(left_ok))
    def _():
        rims[0] = jnp.zeros((16, rows3), b16)

    @pl.when(jnp.logical_not(right_ok))
    def _():
        rims[1] = jnp.zeros((16, rows3), b16)

    row, lane = iotas(16, lanes)
    pick_right = ((row < cells_x) & (lane == row * quarter + quarter - 1)).astype(f32).astype(b16)
    pick_left = (
        ((row >= cells_x) & (row < 2 * cells_x) & (lane == (row - cells_x) * quarter))
        .astype(f32)
        .astype(b16)
    )

    order = (0, 2, 1, 3)
    loads[0].wait()
    for c in range(3):
        field = velocity[c].astype(f32)
        rows = [field[:, x, :] for x in range(cells_x)]
        for q in range(nt):
            cut = slice(q * quarter, (q + 1) * quarter)
            piece = jnp.concatenate([r[:, cut] for r in rows], axis=1)
            chunk[order[q], c * snaps : (c + 1) * snaps] = piece.astype(b16)
    for q in range(nt):
        whole_piece = chunk[order[q]].astype(f32)
        first_row = whole_piece[:, :quarter]
        last_row = whole_piece[:, lanes - quarter :]
        edge_low[order[q]] = jnp.concatenate([first_row[:half3], first_row[half3:]], axis=1).astype(b16)
        edge_high[order[q]] = jnp.concatenate([last_row[:half3], last_row[half3:]], axis=1).astype(b16)
    right_of = [dot16(pick_right, chunk[order[q]], (1, 1)) for q in range(nt)]
    left_of = [dot16(pick_left, chunk[order[q]], (1, 1)) for q in range(nt)]
    rim_out[0] = right_of[nt - 1].astype(b16)
    rim_out[1] = left_of[0].astype(b16)
    for q in (1, 2):
        column[order[q]] = (right_of[q - 1] + left_of[q + 1]).astype(b16)

    pl.semaphore_wait(barrier, expected)

    mine2, theirs2 = 2 * odd, 2 - 2 * odd
    spot_near, spot_far = 2 * odd + lax.div(near, 2), 2 - 2 * odd + lax.div(far, 2)

    def chunk_copies():
        return (
            copy(chunk.at[pl.ds(theirs2, 2)], land_pair, chunk_sems.at[0, 0], chunk_sems.at[1, 0], (ix, iy, partner)),
            copy(chunk.at[spot_near], land_far.at[0], chunk_sems.at[0, 1], chunk_sems.at[1, 1], (ix, iy, near)),
            copy(chunk.at[spot_far], land_far.at[1], chunk_sems.at[0, 2], chunk_sems.at[1, 2], (ix, iy, far)),
        )

    def column_copies():
        return (
            copy(column.at[pl.ds(theirs2, 2)], column_pair, column_sems.at[0, 0], column_sems.at[1, 0], (ix, iy, partner)),
            copy(column.at[spot_near], column_far.at[0], column_sems.at[0, 1], column_sems.at[1, 1], (ix, iy, near)),
            copy(column.at[spot_far], column_far.at[1], column_sems.at[0, 2], column_sems.at[1, 2], (ix, iy, far)),
        )

    def edge_copies(source, side, sems, to_x):
        at = pl.ds(128 * side, 128)
        return (
            copy(source.at[pl.ds(mine2, 2)], halo.at[pl.ds(0, 2), :, at], sems.at[0, 0], sems.at[1, 0], (to_x, iy, it)),
            copy(source.at[pl.ds(theirs2, 2)], halo.at[pl.ds(2, 2), :, at], sems.at[0, 1], sems.at[1, 1], (to_x, iy, partner)),
            copy(source.at[spot_near], halo.at[4, :, at], sems.at[0, 2], sems.at[1, 2], (to_x, iy, near)),
            copy(source.at[spot_far], halo.at[5, :, at], sems.at[0, 3], sems.at[1, 3], (to_x, iy, far)),
        )

    def rim_copies():
        return (
            (right_ok, copy(rim_out.at[0], rims.at[0], rim_sems.at[0, 0], rim_sems.at[1, 0], (ix, jnp.minimum(iy + 1, ny - 1), it))),
            (left_ok, copy(rim_out.at[1], rims.at[1], rim_sems.at[0, 1], rim_sems.at[1, 1], (ix, jnp.maximum(iy - 1, 0), it))),
        )

    highs = edge_copies(edge_high, 0, high_sems, jnp.minimum(ix + 1, nx - 1))
    lows = edge_copies(edge_low, 1, low_sems, jnp.maximum(ix - 1, 0))

    def edges(index, act):
        pl.when(can_up)(functools.partial(act, highs[index]))
        pl.when(can_down)(functools.partial(act, lows[index]))

    def start(c):
        c.start()

    for ok, c in rim_copies():
        pl.when(ok)(functools.partial(start, c))
    chunk_copies()[0].start()
    edges(1, start)
    edges(0, start)
    chunk_copies()[1].start()
    chunk_copies()[2].start()
    edges(2, start)
    edges(3, start)

    def halo_wait(index):
        pl.when(can_down)(lambda: highs[index].wait_recv())
        pl.when(can_up)(lambda: lows[index].wait_recv())

    pl.when(left_ok)(lambda: rim_copies()[0][1].wait_recv())
    pl.when(right_ok)(lambda: rim_copies()[1][1].wait_recv())
    column[order[0]] = (rims[0].astype(f32) + left_of[1]).astype(b16)
    column[order[nt - 1]] = (right_of[nt - 2] + rims[1].astype(f32)).astype(b16)
    for c in column_copies():
        c.start()

    row, lane = iotas(lanes, lanes)
    gap = row - lane
    same = row // quarter == lane // quarter
    both = jnp.concatenate(
        [
            signed_half(gap == quarter, gap == -quarter),
            signed_half((gap == 1) & same, (gap == -1) & same),
        ],
        axis=1,
    )
    row, lane = iotas(256, 2 * lanes)
    wide, at = lane // lanes, lax.rem(lane, lanes)
    rise, k = row // 128, lax.rem(row, 128)
    hit = k // quarter == wide
    k = lax.rem(k, quarter)
    outer = signed_half(
        hit & (rise == 1) & (at == k + lanes - quarter), hit & (rise == 0) & (at == k)
    )
    row, lane = iotas(16, lanes)
    rim = signed_half(
        (row >= cells_x) & (row < 2 * cells_x) & (lane == (row - cells_x) * quarter + quarter - 1),
        (row < cells_x) & (lane == row * quarter),
    )

    def strain(block, border, sides):
        inner = dot16(block, both)
        across = dot16(border, outer)
        dx = inner[:, :lanes] + jnp.concatenate([across[:, :lanes], across[:, lanes:]], axis=0)
        dy = inner[:, lanes:] + dot16(sides, rim, (0, 0))
        ux, vx, wx = (dx[i * snaps : (i + 1) * snaps] for i in range(3))
        uy, vy, wy = (dy[i * snaps : (i + 1) * snaps] for i in range(3))
        fields = jnp.concatenate([ux, vy, 0.5 * (uy + vx), 0.5 * wx, 0.5 * wy], axis=1)
        coarse = fields.astype(b16)
        return coarse, (fields - coarse.astype(f32)).astype(b16)

    def keep(block, values):
        at = pl.ds(pl.multiple_of(block * snaps, snaps), snaps)
        coarse_ref[at], fine_ref[at] = values

    def keep_side(block, values):
        at = pl.ds(pl.multiple_of(block * snaps, snaps), snaps)
        side_coarse[at], side_fine[at] = values

    halo_wait(0)
    keep(it, strain(chunk[mine2 + upper], halo[upper], column[mine2 + upper]))
    keep_side(odd, strain(chunk[mine2 + 1 - upper], halo[1 - upper], column[mine2 + 1 - upper]))
    chunk_copies()[0].wait_recv()
    halo_wait(1)
    column_copies()[0].wait_recv()
    keep(partner, strain(land_pair[upper], halo[2 + upper], column_pair[upper]))
    keep_side(1 - odd, strain(land_pair[1 - upper], halo[3 - upper], column_pair[1 - upper]))

    pair = 2 * snaps
    at = pl.ds(pl.multiple_of(upper * pair, pair), pair)
    coarse, fine = coarse_ref[at], fine_ref[at]
    gram = dot16(coarse, jnp.concatenate([coarse, fine], axis=0), (1, 1))
    coarse, fine = side_coarse[...], side_fine[...]
    gram = gram + dot16(coarse, jnp.concatenate([coarse, fine], axis=0), (1, 1))
    skew = gram[:, pair:]
    parts_pair[...] = (gram[:, :pair] + (skew + skew.T)).reshape(OWNERS, 8, pair)

    near_rank = odd * plane + place
    wide_rank = lax.rem(it + 3, 4) * plane + place

    def pair_owner(k):
        return (lax.div(lax.rem(k, plane), ny), lax.rem(lax.rem(k, plane), ny), 2 * upper + lax.div(k, plane))

    def cross_owner(k):
        return (lax.div(lax.rem(k, plane), ny), lax.rem(lax.rem(k, plane), ny), lax.rem(lax.div(k, plane) + 1, 4))

    def scatter(level, act):
        rank, owner, parts, landed = (
            (near_rank, pair_owner, parts_pair, landed_pair),
            (wide_rank, cross_owner, parts_cross, landed_cross),
        )[level]
        for j in range(OWNERS):
            k = lax.rem(rank + j, OWNERS)
            c = copy(parts.at[k], landed.at[rank], scatter_sems.at[level, j], scatter_in.at[level], owner(k))
            if j:
                act(c)
            else:
                pl.when(rank >= OWNERS)(functools.partial(act, c))

    def spread(level, act):
        rank, whole = ((near_rank, whole_pair), (wide_rank, whole_cross))[level]
        slot = jnp.minimum(rank, OWNERS - 1) + (0 if level else OWNERS * upper)

        def body(j, carry):
            act(
                copy(
                    whole.at[slot], whole.at[slot], spread_sems.at[level, j], spread_in.at[level],
                    device(lax.rem(me + j, devices)),
                )
            )
            return carry

        @pl.when(rank < OWNERS)
        def _():
            lax.fori_loop(1, devices, body, 0)

    def reduce(level):
        rank, parts, landed = (
            (near_rank, parts_pair, landed_pair),
            (wide_rank, parts_cross, landed_cross),
        )[level]
        members = landed.shape[0]
        slot = jnp.minimum(rank, OWNERS - 1)

        @pl.when(rank < OWNERS)
        def _():
            landed[rank] = parts[slot]
            some = landed.at[pl.ds(0, members - 1)]
            copy(some, some, scatter_sems.at[level, 0], scatter_in.at[level], (ix, iy, partner)).wait_recv()
            summed = jnp.sum(landed[...], axis=0)
            if level:
                whole_cross[slot] = summed
            else:
                whole_pair[OWNERS * upper + slot] = summed

        spread(level, start)

    scatter(0, start)

    for i, t in enumerate((near, far)):
        chunk_copies()[1 + i].wait_recv()
        halo_wait(2 + i)
        column_copies()[1 + i].wait_recv()
        keep(t, strain(land_far[i], halo[4 + i], column_far[i]))
    coarse, fine = coarse_ref[:pair], fine_ref[:pair]
    coarse_high, fine_high = coarse_ref[pair:], fine_ref[pair:]
    gram = dot16(coarse_high, jnp.concatenate([coarse, fine], axis=0), (1, 1))
    crossed = gram[:, :pair] + (gram[:, pair:] + dot16(fine_high, coarse, (1, 1)))
    parts_cross[...] = crossed.reshape(OWNERS, 8, pair)
    scatter(1, start)
    reduce(0)
    reduce(1)

    for c in loads[1:]:
        c.wait()
    first = eye(snaps, snaps) + seeds_first[...].astype(f32) * (0.5 / 512.0)
    stacked = jnp.concatenate([eye(snaps, snaps)] * 2, axis=1) * (2.0**-0.5)
    turns = [
        stacked + seeds_merge[level].astype(f32) * (0.5 / (64.0 * 128.0**0.5)) for level in range(2)
    ]

    @pl.when(near_rank < OWNERS)
    def _():
        some = whole_pair.at[pl.ds(0, 2 * OWNERS - 1)]
        copy(some, some, spread_sems.at[0, 0], spread_in.at[0], (ix, iy, partner)).wait_recv()

    @pl.when(near_rank >= OWNERS)
    def _():
        copy(whole_pair, whole_pair, spread_sems.at[0, 0], spread_in.at[0], (ix, iy, partner)).wait_recv()

    pairs = [whole_pair[u * OWNERS : (u + 1) * OWNERS].reshape(pair, pair) for u in (0, 1)]
    blocks = [
        g[i * snaps : (i + 1) * snaps, i * snaps : (i + 1) * snaps] for g in pairs for i in (0, 1)
    ]
    coefs = first_level(blocks, first)
    weights = middle_level(pairs, (coefs[:2], coefs[2:]), turns[0])

    @pl.when(wide_rank < OWNERS)
    def _():
        some = whole_cross.at[pl.ds(0, OWNERS - 1)]
        copy(some, some, spread_sems.at[1, 0], spread_in.at[1], (ix, iy, partner)).wait_recv()

    @pl.when(wide_rank >= OWNERS)
    def _():
        copy(whole_cross, whole_cross, spread_sems.at[1, 0], spread_in.at[1], (ix, iy, partner)).wait_recv()

    weight_ref[...] = last_level(pairs, whole_cross[...].reshape(pair, pair), weights, turns[1])

    def finish(c):
        c.wait_send()

    for ok, c in rim_copies():
        pl.when(ok)(functools.partial(finish, c))
    for c in chunk_copies() + column_copies():
        finish(c)
    for index in range(4):
        edges(index, finish)
    for level in range(2):
        scatter(level, finish)
        spread(level, finish)


def tail_kernel(weight_ref, coarse_ref, fine_ref, out_hbm, out, sem):
    modes, lanes = weight_ref.shape[0], coarse_ref.shape[1]
    weights = weight_ref[...]
    coarse = weights.astype(jnp.bfloat16)
    fine = (weights - coarse.astype(jnp.float32)).astype(jnp.bfloat16)
    both = dot16(jnp.concatenate([coarse, fine], axis=0), coarse_ref[...])
    basis = both[:modes] + (both[modes:] + dot16(coarse, fine_ref[...]))
    quarter = out.shape[1]
    strips = lanes // quarter
    for i in range(strips):
        out[pl.ds(i, modes, stride=strips), :] = basis[:, i * quarter : (i + 1) * quarter]
    done = pltpu.make_async_copy(out, out_hbm, sem)
    done.start()
    done.wait()


def local(velocity, seeds_first, seeds_merge):
    comps, width, cells_x, cells_y = velocity.shape
    nx, ny, nt = (lax.axis_size(a) for a in ("sx", "sy", "ta"))
    quarter = cells_y // nt
    lanes = cells_x * quarter
    plane = nx * ny
    rows3 = comps * width
    pair = 2 * width
    vmem = pl.BlockSpec(memory_space=pltpu.VMEM)
    hbm = pl.BlockSpec(memory_space=pltpu.HBM)
    b16, f32 = jnp.bfloat16, jnp.float32
    dma = pltpu.SemaphoreType.DMA
    coarse, fine, weights = pl.pallas_call(
        functools.partial(gather_kernel, quarter, nx, ny, nt),
        out_shape=(
            jax.ShapeDtypeStruct((nt * width, 5 * lanes), b16),
            jax.ShapeDtypeStruct((nt * width, 5 * lanes), b16),
            jax.ShapeDtypeStruct((width, nt * width), f32),
        ),
        in_specs=[hbm] * 3,
        out_specs=(vmem,) * 3,
        scratch_shapes=[
            pltpu.VMEM(velocity.shape, b16),
            pltpu.VMEM((width, width), jnp.int32),
            pltpu.VMEM((2, width, pair), jnp.int32),
            pltpu.VMEM((nt, rows3, lanes), b16),
            pltpu.VMEM((nt, rows3 // 2, 128), b16),
            pltpu.VMEM((nt, rows3 // 2, 128), b16),
            pltpu.VMEM((nt, 16, rows3), b16),
            pltpu.VMEM((2, 16, rows3), b16),
            pltpu.VMEM((2, 16, rows3), b16),
            pltpu.VMEM((2, rows3, lanes), b16),
            pltpu.VMEM((2, rows3, lanes), b16),
            pltpu.VMEM((2, 16, rows3), b16),
            pltpu.VMEM((2, 16, rows3), b16),
            pltpu.VMEM((6, rows3 // 2, 256), b16),
            pltpu.VMEM((pair, 5 * lanes), b16),
            pltpu.VMEM((pair, 5 * lanes), b16),
            pltpu.VMEM((OWNERS, 8, pair), f32),
            pltpu.VMEM((OWNERS, 8, pair), f32),
            pltpu.VMEM((2 * plane, 8, pair), f32),
            pltpu.VMEM((nt * plane, 8, pair), f32),
            pltpu.VMEM((2 * OWNERS, 8, pair), f32),
            pltpu.VMEM((OWNERS, 8, pair), f32),
            dma((3,)),
            dma((2, 3)),
            dma((2, 3)),
            dma((2, 2)),
            dma((2, 4)),
            dma((2, 4)),
            dma((2, OWNERS)),
            dma((2,)),
            dma((2, nt * plane)),
            dma((2,)),
        ],
        compiler_params=pltpu.CompilerParams(
            collective_id=0, has_side_effects=True, vmem_limit_bytes=40 * 2**20
        ),
        name="gather",
    )(*(pltpu.with_memory_space_constraint(a, pltpu.HBM) for a in (velocity, seeds_first, seeds_merge.transpose(0, 2, 1))))
    strips = 5 * cells_x
    out = pl.pallas_call(
        tail_kernel,
        out_shape=jax.ShapeDtypeStruct((width * strips, quarter), f32),
        in_specs=[vmem] * 3,
        out_specs=hbm,
        scratch_shapes=[pltpu.VMEM((width * strips, quarter), f32), dma],
        compiler_params=pltpu.CompilerParams(vmem_limit_bytes=32 * 2**20),
        name="tail",
    )(weights, coarse, fine)
    return out.reshape(width, 5, cells_x, quarter)


def solution(mesh):
    in_specs = (P(None, "ta", "sx", "sy"), P(), P())
    out_specs = P(None, None, "sx", ("sy", "ta"))
    return jax.shard_map(local, mesh=mesh, in_specs=in_specs, out_specs=out_specs, check_vma=False)
```

```python
import functools

import jax
import jax.numpy as jnp
from jax import lax
from jax.experimental import pallas as pl
from jax.experimental.pallas import tpu as pltpu
from jax.sharding import PartitionSpec as P

HI = lax.Precision.HIGHEST
MESH = pl.DeviceIdType.MESH
OWNERS = 24


def mm(left, right, contract=(1, 0)):
    return lax.dot_general(
        left,
        right,
        (((contract[0],), (contract[1],)), ((), ())),
        precision=HI,
        preferred_element_type=jnp.float32,
    )


def dot16(left, right, contract=(1, 0)):
    return lax.dot_general(
        left,
        right,
        (((contract[0],), (contract[1],)), ((), ())),
        preferred_element_type=jnp.float32,
    )


def iotas(rows, cols):
    return (
        lax.broadcasted_iota(jnp.int32, (rows, cols), 0),
        lax.broadcasted_iota(jnp.int32, (rows, cols), 1),
    )


def eye(rows, cols):
    row, col = iotas(rows, cols)
    return (row == col).astype(jnp.float32)


def signed_half(plus, minus):
    return (0.5 * plus.astype(jnp.float32) - 0.5 * minus.astype(jnp.float32)).astype(jnp.bfloat16)


def eliminate(mats, sides):
    n = mats[0].shape[0]
    batch = len(mats)
    tiles = n // 8
    width = 2 * n
    work = [
        [jnp.concatenate([m, s], axis=1)[8 * i : 8 * i + 8] for i in range(tiles)]
        for m, s in zip(mats, sides)
    ]
    sub = lax.broadcasted_iota(jnp.int32, (8, width), 0)
    done = [[None] * tiles for _ in range(batch)]
    for p in range(tiles):
        cols = [
            [
                [
                    jnp.broadcast_to(work[b][i][:, 8 * p + k : 8 * p + k + 1], (8, width))
                    for i in range(p, tiles)
                ]
                for k in range(8)
            ]
            for b in range(batch)
        ]
        for b in range(batch):
            head = work[b][p]
            rest = [work[b][i] for i in range(p + 1, tiles)]
            scales = jnp.zeros((8, width), jnp.float32)
            for k in range(8):
                pivot = cols[b][k][0][k : k + 1]
                inv = 1.0 / pivot
                scales = jnp.where(sub == k, jnp.broadcast_to(inv, (8, width)), scales)
                row = head[k : k + 1] * inv
                across = [cols[b][j][0][k : k + 1] * inv for j in range(k + 1, 8)]
                below = jnp.where(sub > k, cols[b][k][0], 0.0)
                head = head - below * row
                for j in range(k + 1, 8):
                    cols[b][j][0] = cols[b][j][0] - below * across[j - k - 1]
                for i in range(1, tiles - p):
                    factor = cols[b][k][i]
                    rest[i - 1] = rest[i - 1] - factor * row
                    for j in range(k + 1, 8):
                        cols[b][j][i] = cols[b][j][i] - factor * across[j - k - 1]
            done[b][p] = head * jnp.sqrt(scales)
            for i in range(p + 1, tiles):
                work[b][i] = rest[i - p - 1]
    return [jnp.concatenate(done[b], axis=0)[:, n:] for b in range(batch)]


def total(entries):
    return jnp.sum(jnp.sum(entries, axis=0, keepdims=True), axis=1, keepdims=True)


def first_level(grams, first):
    width = first.shape[0]
    ident = eye(width, width)
    images = [mm(first, g, (0, 0)) for g in grams]
    reduced = [mm(z, first) for z in images]
    solved = eliminate(reduced, images)
    return [c * lax.rsqrt(total(g * ident) / width) for c, g in zip(solved, grams)]


def middle_level(pairs, coefs, turn):
    width = turn.shape[0]
    ident = eye(width, width)
    reduced, sides, scales = [], [], []
    for gram, (low, high) in zip(pairs, coefs):
        lean = jnp.concatenate(
            [mm(low, turn[:, :width], (0, 1)), mm(high, turn[:, width:], (0, 1))], axis=0
        )
        image = mm(lean, gram, (0, 0))
        reduced.append(mm(image, lean))
        norms = [mm(c, c, (0, 0)) for c in (low, high)]
        sides.append(
            jnp.concatenate([mm(image[:, :width], norms[0]), mm(image[:, width:], norms[1])], axis=1)
        )
        trace = total(norms[0] * gram[:width, :width]) + total(norms[1] * gram[width:, width:])
        scales.append(lax.rsqrt(trace / (2 * width)))
    inverses = eliminate(reduced, [ident] * len(pairs))
    return [mm(inv, s) * k for inv, s, k in zip(inverses, sides, scales)]


def last_level(pairs, cross, weights, turn):
    width = turn.shape[0]
    lean = [mm(weights[u], turn[:, u * width : (u + 1) * width], (0, 1)) for u in (0, 1)]
    image = [mm(lean[u], pairs[u], (0, 0)) for u in (0, 1)]
    norms = [mm(weights[u], weights[u], (0, 0)) for u in (0, 1)]
    up = mm(lean[1], cross, (0, 0))
    down = mm(lean[0], cross, (0, 1))
    mixed = mm(up, lean[0])
    reduced = mm(image[0], lean[0]) + mm(image[1], lean[1]) + (mixed + mixed.T)
    trace = total(norms[0] * pairs[0]) + total(norms[1] * pairs[1])
    sides = jnp.concatenate([mm(image[0] + up, norms[0]), mm(image[1] + down, norms[1])], axis=1)
    inverse = eliminate([reduced], [eye(width, width)])[0]
    return mm(inverse, sides) * lax.rsqrt(trace / (2 * width))


def gather_kernel(
    quarter, nx, ny, nt,
    velocity_hbm, first_hbm, merge_hbm,
    coarse_ref, fine_ref, weight_ref,
    velocity, seeds_first, seeds_merge, chunk, edge_low, edge_high, column, rim_out,
    rims, land, column_in, halo_own, halo,
    own_coarse, own_fine, own_landed, shared, parts, landed, whole,
    load_sems, chunk_sems, column_sems, rim_sems, low_sems, high_sems,
    own_sems, own_in, share_sems, share_in, scatter_sems, scatter_in, spread_sems, spread_in,
):
    ix, iy, it = lax.axis_index("sx"), lax.axis_index("sy"), lax.axis_index("ta")
    plane = nx * ny
    devices = plane * nt
    place = ix * ny + iy
    me = it * plane + place
    rows3, lanes = chunk.shape[1:]
    snaps = rows3 // 3
    cells_x = lanes // quarter
    half3 = rows3 // 2
    partner = it + 1 - 2 * lax.rem(it, 2)
    near, far = lax.rem(it + 2, 4), 3 - it
    b16, f32 = jnp.bfloat16, jnp.float32

    def device(t):
        where = lax.rem(t, plane)
        return (lax.div(where, ny), lax.rem(where, ny), lax.div(t, plane))

    def copy(src, dst, send, recv, target):
        return pltpu.make_async_remote_copy(
            src_ref=src, dst_ref=dst, send_sem=send, recv_sem=recv, device_id=target, device_id_type=MESH
        )

    loads = [
        pltpu.make_async_copy(src, dst, load_sems.at[i])
        for i, (src, dst) in enumerate(
            ((velocity_hbm, velocity), (first_hbm, seeds_first), (merge_hbm, seeds_merge))
        )
    ]
    for c in loads:
        c.start()

    barrier = pltpu.get_barrier_semaphore()

    def greet(target):
        pl.semaphore_signal(barrier, inc=1, device_id=target, device_id_type=MESH)

    def greet_plane(j, carry):
        t = lax.rem(place + j, plane)
        greet((lax.div(t, ny), lax.rem(t, ny), it))
        return carry

    others = (partner, near, far)
    for t in others:
        greet((ix, iy, t))
    can_up, can_down = ix < nx - 1, ix > 0
    for ok, step in ((can_up, 1), (can_down, -1)):
        @pl.when(ok)
        def _():
            for t in others:
                greet((ix + step, iy, t))
    lax.fori_loop(1, plane, greet_plane, 0)
    expected = plane - 1 + 3 + jnp.where(can_up, 3, 0) + jnp.where(can_down, 3, 0)

    right_ok, left_ok = iy + 1 < ny, iy > 0

    @pl.when(jnp.logical_not(can_down))
    def _():
        halo[:, :, :128] = jnp.zeros((3, half3, 128), b16)
        halo_own[:, :, :128] = jnp.zeros((nt, half3, 128), b16)

    @pl.when(jnp.logical_not(can_up))
    def _():
        halo[:, :, 128:] = jnp.zeros((3, half3, 128), b16)
        halo_own[:, :, 128:] = jnp.zeros((nt, half3, 128), b16)

    @pl.when(jnp.logical_not(left_ok))
    def _():
        rims[0] = jnp.zeros((16, rows3), b16)

    @pl.when(jnp.logical_not(right_ok))
    def _():
        rims[1] = jnp.zeros((16, rows3), b16)

    row, lane = iotas(16, lanes)
    pick_right = ((row < cells_x) & (lane == row * quarter + quarter - 1)).astype(f32).astype(b16)
    pick_left = (
        ((row >= cells_x) & (row < 2 * cells_x) & (lane == (row - cells_x) * quarter))
        .astype(f32)
        .astype(b16)
    )

    loads[0].wait()
    for c in range(3):
        field = velocity[c].astype(f32)
        rows = [field[:, x, :] for x in range(cells_x)]
        for q in range(nt):
            cut = slice(q * quarter, (q + 1) * quarter)
            piece = jnp.concatenate([r[:, cut] for r in rows], axis=1)
            chunk[q, c * snaps : (c + 1) * snaps] = piece.astype(b16)
    for q in range(nt):
        whole_piece = chunk[q].astype(f32)
        first_row = whole_piece[:, :quarter]
        last_row = whole_piece[:, lanes - quarter :]
        edge_low[q] = jnp.concatenate([first_row[:half3], first_row[half3:]], axis=1).astype(b16)
        edge_high[q] = jnp.concatenate([last_row[:half3], last_row[half3:]], axis=1).astype(b16)
    right_of = [dot16(pick_right, chunk[q], (1, 1)) for q in range(nt)]
    left_of = [dot16(pick_left, chunk[q], (1, 1)) for q in range(nt)]
    rim_out[0] = right_of[nt - 1].astype(b16)
    rim_out[1] = left_of[0].astype(b16)
    for q in (1, 2):
        column[q] = (right_of[q - 1] + left_of[q + 1]).astype(b16)

    pl.semaphore_wait(barrier, expected)

    def chunk_copy(i):
        t = others[i]
        return copy(chunk.at[t], land.at[i], chunk_sems.at[0, i], chunk_sems.at[1, i], (ix, iy, t))

    def column_copy(i):
        t = others[i]
        return copy(column.at[t], column_in.at[i], column_sems.at[0, i], column_sems.at[1, i], (ix, iy, t))

    def edge_copy(source, side, sems, to_x, i):
        at = pl.ds(128 * side, 128)
        if i < 3:
            t = others[i]
            src, dst = source.at[t], halo.at[i, :, at]
        else:
            t, src, dst = it, source, halo_own.at[:, :, at]
        return copy(src, dst, sems.at[0, i], sems.at[1, i], (to_x, iy, t))

    def rim_copies():
        return (
            (right_ok, copy(rim_out.at[0], rims.at[0], rim_sems.at[0, 0], rim_sems.at[1, 0], (ix, jnp.minimum(iy + 1, ny - 1), it))),
            (left_ok, copy(rim_out.at[1], rims.at[1], rim_sems.at[0, 1], rim_sems.at[1, 1], (ix, jnp.maximum(iy - 1, 0), it))),
        )

    def high(i):
        return edge_copy(edge_high, 0, high_sems, jnp.minimum(ix + 1, nx - 1), i)

    def low(i):
        return edge_copy(edge_low, 1, low_sems, jnp.maximum(ix - 1, 0), i)

    def edges(i, act):
        pl.when(can_up)(lambda: act(high(i)))
        pl.when(can_down)(lambda: act(low(i)))

    def start(c):
        c.start()

    for ok, c in rim_copies():
        pl.when(ok)(functools.partial(start, c))
    edges(3, start)
    for i in (2, 1, 0):
        chunk_copy(i).start()
    for i in (2, 1, 0):
        edges(i, start)

    def halo_wait(i):
        pl.when(can_down)(lambda: high(i).wait_recv())
        pl.when(can_up)(lambda: low(i).wait_recv())

    pl.when(left_ok)(lambda: rim_copies()[0][1].wait_recv())
    pl.when(right_ok)(lambda: rim_copies()[1][1].wait_recv())
    column[0] = (rims[0].astype(f32) + left_of[1]).astype(b16)
    column[nt - 1] = (right_of[nt - 2] + rims[1].astype(f32)).astype(b16)
    for i in (2, 1, 0):
        column_copy(i).start()

    row, lane = iotas(lanes, lanes)
    gap = row - lane
    same = row // quarter == lane // quarter
    both = jnp.concatenate(
        [
            signed_half(gap == quarter, gap == -quarter),
            signed_half((gap == 1) & same, (gap == -1) & same),
        ],
        axis=1,
    )
    row, lane = iotas(256, 2 * lanes)
    wide, at = lane // lanes, lax.rem(lane, lanes)
    rise, k = row // 128, lax.rem(row, 128)
    hit = k // quarter == wide
    k = lax.rem(k, quarter)
    outer = signed_half(
        hit & (rise == 1) & (at == k + lanes - quarter), hit & (rise == 0) & (at == k)
    )
    row, lane = iotas(16, lanes)
    rim = signed_half(
        (row >= cells_x) & (row < 2 * cells_x) & (lane == (row - cells_x) * quarter + quarter - 1),
        (row < cells_x) & (lane == row * quarter),
    )

    def strain(block, border, sides):
        inner = dot16(block, both)
        across = dot16(border, outer)
        dx = inner[:, :lanes] + jnp.concatenate([across[:, :lanes], across[:, lanes:]], axis=0)
        dy = inner[:, lanes:] + dot16(sides, rim, (0, 0))
        ux, vx, wx = (dx[i * snaps : (i + 1) * snaps] for i in range(3))
        uy, vy, wy = (dy[i * snaps : (i + 1) * snaps] for i in range(3))
        fields = jnp.concatenate([ux, vy, 0.5 * (uy + vx), 0.5 * wx, 0.5 * wy], axis=1)
        coarse = fields.astype(b16)
        return coarse, (fields - coarse.astype(f32)).astype(b16)

    def keep(block, values):
        at = pl.ds(pl.multiple_of(block * snaps, snaps), snaps)
        coarse_ref[at], fine_ref[at] = values

    halo_wait(3)
    own = jnp.zeros((snaps, 2 * snaps), f32)
    for q in range(nt):
        coarse, fine = strain(chunk[q], halo_own[q], column[q])
        own_coarse[q], own_fine[q] = coarse, fine
        own = own + dot16(coarse, jnp.concatenate([coarse, fine], axis=0), (1, 1))
    skew = own[:, snaps:]
    own = own[:, :snaps] + (skew + skew.T)
    half = snaps // 2
    own_landed[place] = jnp.concatenate([own[:half], own[half:]], axis=1)

    def own_copies(act):
        def body(j, carry):
            t = lax.rem(place + j, plane)
            act(
                copy(
                    own_landed.at[place], own_landed.at[place], own_sems.at[j], own_in.at[0],
                    (lax.div(t, ny), lax.rem(t, ny), it),
                )
            )
            return carry

        lax.fori_loop(1, plane, body, 0)

    own_copies(start)
    keep(it, (own_coarse[it], own_fine[it]))
    for c in loads[1:]:
        c.wait()
    first = eye(snaps, snaps) + seeds_first[...].astype(f32) * (0.5 / 512.0)
    stacked = jnp.concatenate([eye(snaps, snaps)] * 2, axis=1) * (2.0**-0.5)
    turns = [
        stacked + seeds_merge[level].astype(f32) * (0.5 / (64.0 * 128.0**0.5)) for level in range(2)
    ]
    some = own_landed.at[pl.ds(0, plane - 1)]
    copy(some, some, own_sems.at[0], own_in.at[0], (ix, iy, partner)).wait_recv()
    packed = jnp.sum(own_landed[...], axis=0)
    own = jnp.concatenate([packed[:, :snaps], packed[:, snaps:]], axis=0)
    shared[it] = jnp.concatenate([first_level([own], first)[0], own], axis=1)

    def share_copy(i):
        return copy(shared.at[it], shared.at[it], share_sems.at[i], share_in.at[0], (ix, iy, others[i]))

    for i in range(3):
        share_copy(i).start()

    for i in range(3):
        chunk_copy(i).wait_recv()
        halo_wait(i)
        column_copy(i).wait_recv()
        keep(others[i], strain(land[i], halo[i], column_in[i]))
    pair = 2 * snaps
    coarse, fine = coarse_ref[...], fine_ref[...]
    rhs = jnp.concatenate([coarse[:pair], fine[:pair]], axis=0)
    lower = dot16(coarse[snaps:], rhs, (1, 1))
    lower = lower[:, :pair] + (lower[:, pair:] + dot16(fine[snaps:], coarse[:pair], (1, 1)))
    rhs = jnp.concatenate([coarse[pair : pair + snaps], fine[pair : pair + snaps]], axis=0)
    last = dot16(coarse[pair + snaps :], rhs, (1, 1))
    last = last[:, :snaps] + (
        last[:, snaps:] + dot16(fine[pair + snaps :], coarse[pair : pair + snaps], (1, 1))
    )
    rows = jnp.concatenate([lower[snaps:], jnp.concatenate([lower[:snaps, :snaps], last], axis=1)], axis=0)
    parts[...] = rows.reshape(OWNERS, 8, pair)

    rank = jnp.where(it == 0, 2, jnp.where(it == 3, 3, it - 1)) * plane + place
    owner = rank < OWNERS
    slot = jnp.minimum(rank, OWNERS - 1)

    def scatter(act):
        for j in range(OWNERS):
            k = lax.rem(rank + j, OWNERS)
            group, where = lax.div(k, plane), lax.rem(k, plane)
            level = jnp.where(group == 2, 0, jnp.where(group == 3, 3, group + 1))
            c = copy(
                parts.at[k], landed.at[rank], scatter_sems.at[j], scatter_in.at[0],
                (lax.div(where, ny), lax.rem(where, ny), level),
            )
            if j:
                act(c)
            else:
                pl.when(jnp.logical_not(owner))(functools.partial(act, c))

    def spread(act):
        def body(j, carry):
            act(
                copy(
                    whole.at[slot], whole.at[slot], spread_sems.at[j], spread_in.at[0],
                    device(lax.rem(me + j, devices)),
                )
            )
            return carry

        @pl.when(owner)
        def _():
            lax.fori_loop(1, devices, body, 0)

    scatter(start)

    @pl.when(owner)
    def _():
        landed[rank] = parts[slot]
        some = landed.at[pl.ds(0, devices - 1)]
        copy(some, some, scatter_sems.at[0], scatter_in.at[0], (ix, iy, partner)).wait_recv()
        whole[slot] = jnp.sum(landed[...], axis=0)

    spread(start)
    some = shared.at[pl.ds(0, nt - 1)]
    copy(some, some, share_sems.at[0], share_in.at[0], (ix, iy, partner)).wait_recv()
    coefs = [shared[b][:, :snaps] for b in range(nt)]
    grams = [shared[b][:, snaps:] for b in range(nt)]

    @pl.when(owner)
    def _():
        some = whole.at[pl.ds(0, OWNERS - 1)]
        copy(some, some, spread_sems.at[0], spread_in.at[0], (ix, iy, partner)).wait_recv()

    @pl.when(jnp.logical_not(owner))
    def _():
        copy(whole, whole, spread_sems.at[0], spread_in.at[0], (ix, iy, partner)).wait_recv()

    rows = whole[...].reshape(OWNERS * 8, pair)
    cross = rows[:pair]
    pairs = []
    for u in range(2):
        mixed = rows[pair:, u * snaps : (u + 1) * snaps]
        pairs.append(
            jnp.concatenate(
                [
                    jnp.concatenate([grams[2 * u], mixed.T], axis=1),
                    jnp.concatenate([mixed, grams[2 * u + 1]], axis=1),
                ],
                axis=0,
            )
        )
    weights = middle_level(pairs, (coefs[:2], coefs[2:]), turns[0])
    weight_ref[...] = last_level(pairs, cross, weights, turns[1])

    def finish(c):
        c.wait_send()

    for ok, c in rim_copies():
        pl.when(ok)(functools.partial(finish, c))
    for i in range(3):
        finish(chunk_copy(i))
        finish(column_copy(i))
        finish(share_copy(i))
    for i in range(4):
        edges(i, finish)
    own_copies(finish)
    scatter(finish)
    spread(finish)


def tail_kernel(weight_ref, coarse_ref, fine_ref, out_hbm, out, sem):
    modes, lanes = weight_ref.shape[0], coarse_ref.shape[1]
    weights = weight_ref[...]
    coarse = weights.astype(jnp.bfloat16)
    fine = (weights - coarse.astype(jnp.float32)).astype(jnp.bfloat16)
    both = dot16(jnp.concatenate([coarse, fine], axis=0), coarse_ref[...])
    basis = both[:modes] + (both[modes:] + dot16(coarse, fine_ref[...]))
    quarter = out.shape[1]
    strips = lanes // quarter
    for i in range(strips):
        out[pl.ds(i, modes, stride=strips), :] = basis[:, i * quarter : (i + 1) * quarter]
    done = pltpu.make_async_copy(out, out_hbm, sem)
    done.start()
    done.wait()


def local(velocity, seeds_first, seeds_merge):
    comps, width, cells_x, cells_y = velocity.shape
    nx, ny, nt = (lax.axis_size(a) for a in ("sx", "sy", "ta"))
    quarter = cells_y // nt
    lanes = cells_x * quarter
    plane = nx * ny
    rows3 = comps * width
    pair = 2 * width
    vmem = pl.BlockSpec(memory_space=pltpu.VMEM)
    hbm = pl.BlockSpec(memory_space=pltpu.HBM)
    b16, f32 = jnp.bfloat16, jnp.float32
    dma = pltpu.SemaphoreType.DMA
    coarse, fine, weights = pl.pallas_call(
        functools.partial(gather_kernel, quarter, nx, ny, nt),
        out_shape=(
            jax.ShapeDtypeStruct((nt * width, 5 * lanes), b16),
            jax.ShapeDtypeStruct((nt * width, 5 * lanes), b16),
            jax.ShapeDtypeStruct((width, nt * width), f32),
        ),
        in_specs=[hbm] * 3,
        out_specs=(vmem,) * 3,
        scratch_shapes=[
            pltpu.VMEM(velocity.shape, b16),
            pltpu.VMEM((width, width), jnp.int32),
            pltpu.VMEM((2, width, pair), jnp.int32),
            pltpu.VMEM((nt, rows3, lanes), b16),
            pltpu.VMEM((nt, rows3 // 2, 128), b16),
            pltpu.VMEM((nt, rows3 // 2, 128), b16),
            pltpu.VMEM((nt, 16, rows3), b16),
            pltpu.VMEM((2, 16, rows3), b16),
            pltpu.VMEM((2, 16, rows3), b16),
            pltpu.VMEM((3, rows3, lanes), b16),
            pltpu.VMEM((3, 16, rows3), b16),
            pltpu.VMEM((nt, rows3 // 2, 256), b16),
            pltpu.VMEM((3, rows3 // 2, 256), b16),
            pltpu.VMEM((nt, width, 5 * lanes), b16),
            pltpu.VMEM((nt, width, 5 * lanes), b16),
            pltpu.VMEM((plane, width // 2, pair), f32),
            pltpu.VMEM((nt, width, pair), f32),
            pltpu.VMEM((OWNERS, 8, pair), f32),
            pltpu.VMEM((nt * plane, 8, pair), f32),
            pltpu.VMEM((OWNERS, 8, pair), f32),
            dma((3,)),
            dma((2, 3)),
            dma((2, 3)),
            dma((2, 2)),
            dma((2, 4)),
            dma((2, 4)),
            dma((plane,)),
            dma((1,)),
            dma((3,)),
            dma((1,)),
            dma((OWNERS,)),
            dma((1,)),
            dma((nt * plane,)),
            dma((1,)),
        ],
        compiler_params=pltpu.CompilerParams(
            collective_id=0, has_side_effects=True, vmem_limit_bytes=40 * 2**20
        ),
        name="gather",
    )(*(pltpu.with_memory_space_constraint(a, pltpu.HBM) for a in (velocity, seeds_first, seeds_merge.transpose(0, 2, 1))))
    strips = 5 * cells_x
    out = pl.pallas_call(
        tail_kernel,
        out_shape=jax.ShapeDtypeStruct((width * strips, quarter), f32),
        in_specs=[vmem] * 3,
        out_specs=hbm,
        scratch_shapes=[pltpu.VMEM((width * strips, quarter), f32), dma],
        compiler_params=pltpu.CompilerParams(vmem_limit_bytes=32 * 2**20),
        name="tail",
    )(weights, coarse, fine)
    return out.reshape(width, 5, cells_x, quarter)


def solution(mesh):
    in_specs = (P(None, "ta", "sx", "sy"), P(), P())
    out_specs = P(None, None, "sx", ("sy", "ta"))
    return jax.shard_map(local, mesh=mesh, in_specs=in_specs, out_specs=out_specs, check_vma=False)
```

```python
import functools

import jax
import jax.numpy as jnp
from jax import lax
from jax.experimental import pallas as pl
from jax.experimental.pallas import tpu as pltpu
from jax.sharding import PartitionSpec as P

HI = lax.Precision.HIGHEST
MESH = pl.DeviceIdType.MESH
OWNERS = 24
LEAD = 8


def mm(left, right, contract=(1, 0)):
    return lax.dot_general(
        left,
        right,
        (((contract[0],), (contract[1],)), ((), ())),
        precision=HI,
        preferred_element_type=jnp.float32,
    )


def dot16(left, right, contract=(1, 0)):
    return lax.dot_general(
        left,
        right,
        (((contract[0],), (contract[1],)), ((), ())),
        preferred_element_type=jnp.float32,
    )


def iotas(rows, cols):
    return (
        lax.broadcasted_iota(jnp.int32, (rows, cols), 0),
        lax.broadcasted_iota(jnp.int32, (rows, cols), 1),
    )


def eye(rows, cols):
    row, col = iotas(rows, cols)
    return (row == col).astype(jnp.float32)


def signed_half(plus, minus):
    return (0.5 * plus.astype(jnp.float32) - 0.5 * minus.astype(jnp.float32)).astype(jnp.bfloat16)


def eliminate(mats, sides):
    n = mats[0].shape[0]
    batch = len(mats)
    tiles = n // 8
    width = 2 * n
    work = [
        [jnp.concatenate([m, s], axis=1)[8 * i : 8 * i + 8] for i in range(tiles)]
        for m, s in zip(mats, sides)
    ]
    sub = lax.broadcasted_iota(jnp.int32, (8, width), 0)
    done = [[None] * tiles for _ in range(batch)]
    for p in range(tiles):
        cols = [
            [
                [
                    jnp.broadcast_to(work[b][i][:, 8 * p + k : 8 * p + k + 1], (8, width))
                    for i in range(p, tiles)
                ]
                for k in range(8)
            ]
            for b in range(batch)
        ]
        for b in range(batch):
            head = work[b][p]
            rest = [work[b][i] for i in range(p + 1, tiles)]
            scales = jnp.zeros((8, width), jnp.float32)
            for k in range(8):
                pivot = cols[b][k][0][k : k + 1]
                inv = 1.0 / pivot
                scales = jnp.where(sub == k, jnp.broadcast_to(inv, (8, width)), scales)
                row = head[k : k + 1] * inv
                across = [cols[b][j][0][k : k + 1] * inv for j in range(k + 1, 8)]
                below = jnp.where(sub > k, cols[b][k][0], 0.0)
                head = head - below * row
                for j in range(k + 1, 8):
                    cols[b][j][0] = cols[b][j][0] - below * across[j - k - 1]
                for i in range(1, tiles - p):
                    factor = cols[b][k][i]
                    rest[i - 1] = rest[i - 1] - factor * row
                    for j in range(k + 1, 8):
                        cols[b][j][i] = cols[b][j][i] - factor * across[j - k - 1]
            done[b][p] = head * jnp.sqrt(scales)
            for i in range(p + 1, tiles):
                work[b][i] = rest[i - p - 1]
    return [jnp.concatenate(done[b], axis=0)[:, n:] for b in range(batch)]


def total(entries):
    return jnp.sum(jnp.sum(entries, axis=0, keepdims=True), axis=1, keepdims=True)


def first_level(grams, first):
    width = first.shape[0]
    ident = eye(width, width)
    images = [mm(first, g, (0, 0)) for g in grams]
    reduced = [mm(z, first) for z in images]
    solved = eliminate(reduced, images)
    return [c * lax.rsqrt(total(g * ident) / width) for c, g in zip(solved, grams)]


def prepare(coefs, turn):
    width = turn.shape[0]
    lean = [mm(c, turn[:, i * width : (i + 1) * width], (0, 1)) for i, c in enumerate(coefs)]
    return jnp.concatenate(lean, axis=0), [mm(c, c, (0, 0)) for c in coefs]


def middle_level(pairs, ready):
    width = pairs[0].shape[0] // 2
    reduced, sides, scales = [], [], []
    for gram, (lean, norms) in zip(pairs, ready):
        image = mm(lean, gram, (0, 0))
        reduced.append(mm(image, lean))
        sides.append(
            jnp.concatenate([mm(image[:, :width], norms[0]), mm(image[:, width:], norms[1])], axis=1)
        )
        trace = total(norms[0] * gram[:width, :width]) + total(norms[1] * gram[width:, width:])
        scales.append(lax.rsqrt(trace / (2 * width)))
    inverses = eliminate(reduced, [eye(width, width)] * len(pairs))
    return [mm(inv, s) * k for inv, s, k in zip(inverses, sides, scales)]


def last_level(pairs, cross, weights, turn):
    width = turn.shape[0]
    lean = [mm(weights[u], turn[:, u * width : (u + 1) * width], (0, 1)) for u in (0, 1)]
    image = [mm(lean[u], pairs[u], (0, 0)) for u in (0, 1)]
    norms = [mm(weights[u], weights[u], (0, 0)) for u in (0, 1)]
    up = mm(lean[1], cross, (0, 0))
    down = mm(lean[0], cross, (0, 1))
    mixed = mm(up, lean[0])
    reduced = mm(image[0], lean[0]) + mm(image[1], lean[1]) + (mixed + mixed.T)
    trace = total(norms[0] * pairs[0]) + total(norms[1] * pairs[1])
    sides = jnp.concatenate([mm(image[0] + up, norms[0]), mm(image[1] + down, norms[1])], axis=1)
    inverse = eliminate([reduced], [eye(width, width)])[0]
    return mm(inverse, sides) * lax.rsqrt(trace / (2 * width))


def gather_kernel(
    quarter, nx, ny, nt,
    velocity_hbm, first_hbm, merge_hbm,
    coarse_ref, fine_ref, weight_ref,
    velocity, seeds_first, seeds_merge, chunk, edge_low, edge_high, column, rim_out,
    rims, land, column_in, halo_own, halo,
    own_coarse, own_fine, own_landed, shared, parts, landed, whole,
    load_sems, chunk_sems, column_sems, rim_sems, low_sems, high_sems,
    own_sems, own_in, share_sems, share_in, scatter_sems, scatter_in, spread_sems, spread_in,
):
    ix, iy, it = lax.axis_index("sx"), lax.axis_index("sy"), lax.axis_index("ta")
    plane = nx * ny
    devices = plane * nt
    place = ix * ny + iy
    me = it * plane + place
    rows3, lanes = chunk.shape[1:]
    snaps = rows3 // 3
    cells_x = lanes // quarter
    half3 = rows3 // 2
    partner = it + 1 - 2 * lax.rem(it, 2)
    near, far = lax.rem(it + 2, 4), 3 - it
    b16, f32 = jnp.bfloat16, jnp.float32

    def device(t):
        where = lax.rem(t, plane)
        return (lax.div(where, ny), lax.rem(where, ny), lax.div(t, plane))

    def copy(src, dst, send, recv, target):
        return pltpu.make_async_remote_copy(
            src_ref=src, dst_ref=dst, send_sem=send, recv_sem=recv, device_id=target, device_id_type=MESH
        )

    loads = [
        pltpu.make_async_copy(src, dst, load_sems.at[i])
        for i, (src, dst) in enumerate(
            ((velocity_hbm, velocity), (first_hbm, seeds_first), (merge_hbm, seeds_merge))
        )
    ]
    for c in loads:
        c.start()

    barrier = pltpu.get_barrier_semaphore()

    def greet(target):
        pl.semaphore_signal(barrier, inc=1, device_id=target, device_id_type=MESH)

    def greet_plane(j, carry):
        t = lax.rem(place + j, plane)
        greet((lax.div(t, ny), lax.rem(t, ny), it))
        return carry

    others = (partner, near, far)
    for t in others:
        greet((ix, iy, t))
    can_up, can_down = ix < nx - 1, ix > 0
    for ok, step in ((can_up, 1), (can_down, -1)):
        @pl.when(ok)
        def _():
            for t in others:
                greet((ix + step, iy, t))
    lax.fori_loop(1, plane, greet_plane, 0)
    expected = plane - 1 + 3 + jnp.where(can_up, 3, 0) + jnp.where(can_down, 3, 0)

    right_ok, left_ok = iy + 1 < ny, iy > 0

    @pl.when(jnp.logical_not(can_down))
    def _():
        halo[:, :, :128] = jnp.zeros((3, half3, 128), b16)
        halo_own[:, :, :128] = jnp.zeros((nt, half3, 128), b16)

    @pl.when(jnp.logical_not(can_up))
    def _():
        halo[:, :, 128:] = jnp.zeros((3, half3, 128), b16)
        halo_own[:, :, 128:] = jnp.zeros((nt, half3, 128), b16)

    @pl.when(jnp.logical_not(left_ok))
    def _():
        rims[0] = jnp.zeros((16, rows3), b16)

    @pl.when(jnp.logical_not(right_ok))
    def _():
        rims[1] = jnp.zeros((16, rows3), b16)

    row, lane = iotas(16, lanes)
    pick_right = ((row < cells_x) & (lane == row * quarter + quarter - 1)).astype(f32).astype(b16)
    pick_left = (
        ((row >= cells_x) & (row < 2 * cells_x) & (lane == (row - cells_x) * quarter))
        .astype(f32)
        .astype(b16)
    )

    loads[0].wait()
    for c in range(3):
        field = velocity[c].astype(f32)
        rows = [field[:, x, :] for x in range(cells_x)]
        for q in range(nt):
            cut = slice(q * quarter, (q + 1) * quarter)
            piece = jnp.concatenate([r[:, cut] for r in rows], axis=1)
            chunk[q, c * snaps : (c + 1) * snaps] = piece.astype(b16)
    for q in range(nt):
        whole_piece = chunk[q].astype(f32)
        first_row = whole_piece[:, :quarter]
        last_row = whole_piece[:, lanes - quarter :]
        edge_low[q] = jnp.concatenate([first_row[:half3], first_row[half3:]], axis=1).astype(b16)
        edge_high[q] = jnp.concatenate([last_row[:half3], last_row[half3:]], axis=1).astype(b16)
    right_of = [dot16(pick_right, chunk[q], (1, 1)) for q in range(nt)]
    left_of = [dot16(pick_left, chunk[q], (1, 1)) for q in range(nt)]
    rim_out[0] = right_of[nt - 1].astype(b16)
    rim_out[1] = left_of[0].astype(b16)
    for q in (1, 2):
        column[q] = (right_of[q - 1] + left_of[q + 1]).astype(b16)

    pl.semaphore_wait(barrier, expected)

    def chunk_copy(i):
        t = others[i]
        return copy(chunk.at[t], land.at[i], chunk_sems.at[0, i], chunk_sems.at[1, i], (ix, iy, t))

    def column_copy(i):
        t = others[i]
        return copy(column.at[t], column_in.at[i], column_sems.at[0, i], column_sems.at[1, i], (ix, iy, t))

    def edge_copy(source, side, sems, to_x, i):
        at = pl.ds(128 * side, 128)
        if i < 3:
            t = others[i]
            src, dst = source.at[t], halo.at[i, :, at]
        else:
            t, src, dst = it, source, halo_own.at[:, :, at]
        return copy(src, dst, sems.at[0, i], sems.at[1, i], (to_x, iy, t))

    def rim_copies():
        return (
            (right_ok, copy(rim_out.at[0], rims.at[0], rim_sems.at[0, 0], rim_sems.at[1, 0], (ix, jnp.minimum(iy + 1, ny - 1), it))),
            (left_ok, copy(rim_out.at[1], rims.at[1], rim_sems.at[0, 1], rim_sems.at[1, 1], (ix, jnp.maximum(iy - 1, 0), it))),
        )

    def high(i):
        return edge_copy(edge_high, 0, high_sems, jnp.minimum(ix + 1, nx - 1), i)

    def low(i):
        return edge_copy(edge_low, 1, low_sems, jnp.maximum(ix - 1, 0), i)

    def edges(i, act):
        pl.when(can_up)(lambda: act(high(i)))
        pl.when(can_down)(lambda: act(low(i)))

    def start(c):
        c.start()

    for ok, c in rim_copies():
        pl.when(ok)(functools.partial(start, c))
    edges(3, start)
    for i in (2, 1, 0):
        chunk_copy(i).start()
    for i in (2, 1, 0):
        edges(i, start)

    def halo_wait(i):
        pl.when(can_down)(lambda: high(i).wait_recv())
        pl.when(can_up)(lambda: low(i).wait_recv())

    pl.when(left_ok)(lambda: rim_copies()[0][1].wait_recv())
    pl.when(right_ok)(lambda: rim_copies()[1][1].wait_recv())
    column[0] = (rims[0].astype(f32) + left_of[1]).astype(b16)
    column[nt - 1] = (right_of[nt - 2] + rims[1].astype(f32)).astype(b16)
    for i in (2, 1, 0):
        column_copy(i).start()

    row, lane = iotas(lanes, lanes)
    gap = row - lane
    same = row // quarter == lane // quarter
    both = jnp.concatenate(
        [
            signed_half(gap == quarter, gap == -quarter),
            signed_half((gap == 1) & same, (gap == -1) & same),
        ],
        axis=1,
    )
    row, lane = iotas(256, 2 * lanes)
    wide, at = lane // lanes, lax.rem(lane, lanes)
    rise, k = row // 128, lax.rem(row, 128)
    hit = k // quarter == wide
    k = lax.rem(k, quarter)
    outer = signed_half(
        hit & (rise == 1) & (at == k + lanes - quarter), hit & (rise == 0) & (at == k)
    )
    row, lane = iotas(16, lanes)
    rim = signed_half(
        (row >= cells_x) & (row < 2 * cells_x) & (lane == (row - cells_x) * quarter + quarter - 1),
        (row < cells_x) & (lane == row * quarter),
    )

    def strain(block, border, sides):
        inner = dot16(block, both)
        across = dot16(border, outer)
        dx = inner[:, :lanes] + jnp.concatenate([across[:, :lanes], across[:, lanes:]], axis=0)
        dy = inner[:, lanes:] + dot16(sides, rim, (0, 0))
        ux, vx, wx = (dx[i * snaps : (i + 1) * snaps] for i in range(3))
        uy, vy, wy = (dy[i * snaps : (i + 1) * snaps] for i in range(3))
        fields = jnp.concatenate([ux, vy, 0.5 * (uy + vx), 0.5 * wx, 0.5 * wy], axis=1)
        coarse = fields.astype(b16)
        return coarse, (fields - coarse.astype(f32)).astype(b16)

    def keep(block, values):
        at = pl.ds(pl.multiple_of(block * snaps, snaps), snaps)
        coarse_ref[at], fine_ref[at] = values

    halo_wait(3)
    own = jnp.zeros((snaps, 2 * snaps), f32)
    for q in range(nt):
        coarse, fine = strain(chunk[q], halo_own[q], column[q])
        own_coarse[q], own_fine[q] = coarse, fine
        own = own + dot16(coarse, jnp.concatenate([coarse, fine], axis=0), (1, 1))
    skew = own[:, snaps:]
    own = own[:, :snaps] + (skew + skew.T)
    half = snaps // 2
    own_landed[place] = jnp.concatenate([own[:half], own[half:]], axis=1)

    def own_copies(act):
        def body(j, carry):
            t = lax.rem(place + j, plane)
            act(
                copy(
                    own_landed.at[place], own_landed.at[place], own_sems.at[j], own_in.at[0],
                    (lax.div(t, ny), lax.rem(t, ny), it),
                )
            )
            return carry

        lax.fori_loop(1, plane, body, 0)

    own_copies(start)
    keep(it, (own_coarse[it], own_fine[it]))
    for c in loads[1:]:
        c.wait()
    first = eye(snaps, snaps) + seeds_first[...].astype(f32) * (0.5 / 512.0)
    stacked = jnp.concatenate([eye(snaps, snaps)] * 2, axis=1) * (2.0**-0.5)
    turns = [
        stacked + seeds_merge[level].astype(f32) * (0.5 / (64.0 * 128.0**0.5)) for level in range(2)
    ]
    some = own_landed.at[pl.ds(0, plane - 1)]
    copy(some, some, own_sems.at[0], own_in.at[0], (ix, iy, partner)).wait_recv()
    packed = jnp.sum(own_landed[...], axis=0)
    own = jnp.concatenate([packed[:, :snaps], packed[:, snaps:]], axis=0)
    shared[it] = jnp.concatenate([first_level([own], first)[0], own], axis=1)

    def share_copy(i):
        return copy(shared.at[it], shared.at[it], share_sems.at[i], share_in.at[0], (ix, iy, others[i]))

    for i in range(3):
        share_copy(i).start()

    for i in range(3):
        chunk_copy(i).wait_recv()
        halo_wait(i)
        column_copy(i).wait_recv()
        keep(others[i], strain(land[i], halo[i], column_in[i]))
    pair = 2 * snaps
    coarse, fine = coarse_ref[...], fine_ref[...]
    rhs = jnp.concatenate([coarse[:pair], fine[:pair]], axis=0)
    lower = dot16(coarse[snaps:], rhs, (1, 1))
    lower = lower[:, :pair] + (lower[:, pair:] + dot16(fine[snaps:], coarse[:pair], (1, 1)))
    rhs = jnp.concatenate([coarse[pair : pair + snaps], fine[pair : pair + snaps]], axis=0)
    last = dot16(coarse[pair + snaps :], rhs, (1, 1))
    last = last[:, :snaps] + (
        last[:, snaps:] + dot16(fine[pair + snaps :], coarse[pair : pair + snaps], (1, 1))
    )
    rows = jnp.concatenate([jnp.concatenate([lower[:snaps, :snaps], last], axis=1), lower[snaps:]], axis=0)
    parts[...] = rows.reshape(OWNERS, 8, pair)

    rank = jnp.where(it == 0, 2, jnp.where(it == 3, 3, it - 1)) * plane + place
    owner = rank < OWNERS
    slot = jnp.minimum(rank, OWNERS - 1)

    def scatter(act):
        for j in range(OWNERS):
            if j < LEAD:
                k = lax.rem(place + j, LEAD)
            else:
                k = LEAD + lax.rem(place + j, OWNERS - LEAD)
            group, where = lax.div(k, plane), lax.rem(k, plane)
            level = jnp.where(group == 2, 0, jnp.where(group == 3, 3, group + 1))
            c = copy(
                parts.at[k], landed.at[rank], scatter_sems.at[j], scatter_in.at[0],
                (lax.div(where, ny), lax.rem(where, ny), level),
            )
            pl.when(rank != k)(functools.partial(act, c))

    lead = slot < LEAD

    def spread(act):
        def body(t, carry):
            c = copy(
                whole.at[slot], whole.at[slot], spread_sems.at[t], spread_in.at[jnp.where(lead, 0, 1)],
                device(t),
            )
            pl.when(t != me)(functools.partial(act, c))
            return carry

        @pl.when(owner)
        def _():
            lax.fori_loop(0, devices, body, 0)

    scatter(start)

    @pl.when(owner)
    def _():
        landed[rank] = parts[slot]
        some = landed.at[pl.ds(0, devices - 1)]
        copy(some, some, scatter_sems.at[0], scatter_in.at[0], (ix, iy, partner)).wait_recv()
        whole[slot] = jnp.sum(landed[...], axis=0)

    spread(start)
    some = shared.at[pl.ds(0, nt - 1)]
    copy(some, some, share_sems.at[0], share_in.at[0], (ix, iy, partner)).wait_recv()
    coefs = [shared[b][:, :snaps] for b in range(nt)]
    grams = [shared[b][:, snaps:] for b in range(nt)]

    ready = [prepare(coefs[2 * u : 2 * u + 2], turns[0]) for u in range(2)]

    def arrived(part, first_piece, count, own_piece):
        def wait(pieces):
            some = whole.at[pl.ds(first_piece, pieces)]
            copy(some, some, spread_sems.at[0], spread_in.at[part], (ix, iy, partner)).wait_recv()

        pl.when(own_piece)(lambda: wait(count - 1))
        pl.when(jnp.logical_not(own_piece))(lambda: wait(count))
        return whole[first_piece : first_piece + count].reshape(count * 8, pair)

    rows = arrived(0, 0, LEAD, jnp.logical_and(owner, lead))
    pairs = []
    for u in range(2):
        mixed = rows[:, u * snaps : (u + 1) * snaps]
        pairs.append(
            jnp.concatenate(
                [
                    jnp.concatenate([grams[2 * u], mixed.T], axis=1),
                    jnp.concatenate([mixed, grams[2 * u + 1]], axis=1),
                ],
                axis=0,
            )
        )
    weights = middle_level(pairs, ready)
    cross = arrived(1, LEAD, OWNERS - LEAD, jnp.logical_and(owner, jnp.logical_not(lead)))
    weight_ref[...] = last_level(pairs, cross, weights, turns[1])

    def finish(c):
        c.wait_send()

    for ok, c in rim_copies():
        pl.when(ok)(functools.partial(finish, c))
    for i in range(3):
        finish(chunk_copy(i))
        finish(column_copy(i))
        finish(share_copy(i))
    for i in range(4):
        edges(i, finish)
    own_copies(finish)
    scatter(finish)
    spread(finish)


def tail_kernel(weight_ref, coarse_ref, fine_ref, out_hbm, out, sem):
    modes, lanes = weight_ref.shape[0], coarse_ref.shape[1]
    weights = weight_ref[...]
    coarse = weights.astype(jnp.bfloat16)
    fine = (weights - coarse.astype(jnp.float32)).astype(jnp.bfloat16)
    both = dot16(jnp.concatenate([coarse, fine], axis=0), coarse_ref[...])
    basis = both[:modes] + (both[modes:] + dot16(coarse, fine_ref[...]))
    quarter = out.shape[1]
    strips = lanes // quarter
    for i in range(strips):
        out[pl.ds(i, modes, stride=strips), :] = basis[:, i * quarter : (i + 1) * quarter]
    done = pltpu.make_async_copy(out, out_hbm, sem)
    done.start()
    done.wait()


def local(velocity, seeds_first, seeds_merge):
    comps, width, cells_x, cells_y = velocity.shape
    nx, ny, nt = (lax.axis_size(a) for a in ("sx", "sy", "ta"))
    quarter = cells_y // nt
    lanes = cells_x * quarter
    plane = nx * ny
    rows3 = comps * width
    pair = 2 * width
    vmem = pl.BlockSpec(memory_space=pltpu.VMEM)
    hbm = pl.BlockSpec(memory_space=pltpu.HBM)
    b16, f32 = jnp.bfloat16, jnp.float32
    dma = pltpu.SemaphoreType.DMA
    coarse, fine, weights = pl.pallas_call(
        functools.partial(gather_kernel, quarter, nx, ny, nt),
        out_shape=(
            jax.ShapeDtypeStruct((nt * width, 5 * lanes), b16),
            jax.ShapeDtypeStruct((nt * width, 5 * lanes), b16),
            jax.ShapeDtypeStruct((width, nt * width), f32),
        ),
        in_specs=[hbm] * 3,
        out_specs=(vmem,) * 3,
        scratch_shapes=[
            pltpu.VMEM(velocity.shape, b16),
            pltpu.VMEM((width, width), jnp.int32),
            pltpu.VMEM((2, width, pair), jnp.int32),
            pltpu.VMEM((nt, rows3, lanes), b16),
            pltpu.VMEM((nt, rows3 // 2, 128), b16),
            pltpu.VMEM((nt, rows3 // 2, 128), b16),
            pltpu.VMEM((nt, 16, rows3), b16),
            pltpu.VMEM((2, 16, rows3), b16),
            pltpu.VMEM((2, 16, rows3), b16),
            pltpu.VMEM((3, rows3, lanes), b16),
            pltpu.VMEM((3, 16, rows3), b16),
            pltpu.VMEM((nt, rows3 // 2, 256), b16),
            pltpu.VMEM((3, rows3 // 2, 256), b16),
            pltpu.VMEM((nt, width, 5 * lanes), b16),
            pltpu.VMEM((nt, width, 5 * lanes), b16),
            pltpu.VMEM((plane, width // 2, pair), f32),
            pltpu.VMEM((nt, width, pair), f32),
            pltpu.VMEM((OWNERS, 8, pair), f32),
            pltpu.VMEM((nt * plane, 8, pair), f32),
            pltpu.VMEM((OWNERS, 8, pair), f32),
            dma((3,)),
            dma((2, 3)),
            dma((2, 3)),
            dma((2, 2)),
            dma((2, 4)),
            dma((2, 4)),
            dma((plane,)),
            dma((1,)),
            dma((3,)),
            dma((1,)),
            dma((OWNERS,)),
            dma((1,)),
            dma((nt * plane,)),
            dma((2,)),
        ],
        compiler_params=pltpu.CompilerParams(
            collective_id=0, has_side_effects=True, vmem_limit_bytes=40 * 2**20
        ),
        name="gather",
    )(*(pltpu.with_memory_space_constraint(a, pltpu.HBM) for a in (velocity, seeds_first, seeds_merge.transpose(0, 2, 1))))
    strips = 5 * cells_x
    out = pl.pallas_call(
        tail_kernel,
        out_shape=jax.ShapeDtypeStruct((width * strips, quarter), f32),
        in_specs=[vmem] * 3,
        out_specs=hbm,
        scratch_shapes=[pltpu.VMEM((width * strips, quarter), f32), dma],
        compiler_params=pltpu.CompilerParams(vmem_limit_bytes=32 * 2**20),
        name="tail",
    )(weights, coarse, fine)
    return out.reshape(width, 5, cells_x, quarter)


def solution(mesh):
    in_specs = (P(None, "ta", "sx", "sy"), P(), P())
    out_specs = P(None, None, "sx", ("sy", "ta"))
    return jax.shard_map(local, mesh=mesh, in_specs=in_specs, out_specs=out_specs, check_vma=False)
```

```python
import functools

import jax
import jax.numpy as jnp
from jax import lax
from jax.experimental import pallas as pl
from jax.experimental.pallas import tpu as pltpu
from jax.sharding import PartitionSpec as P

HI = lax.Precision.HIGHEST
MESH = pl.DeviceIdType.MESH
OWNERS = 24
LEAD = 8


def mm(left, right, contract=(1, 0)):
    return lax.dot_general(
        left,
        right,
        (((contract[0],), (contract[1],)), ((), ())),
        precision=HI,
        preferred_element_type=jnp.float32,
    )


def dot16(left, right, contract=(1, 0)):
    return lax.dot_general(
        left,
        right,
        (((contract[0],), (contract[1],)), ((), ())),
        preferred_element_type=jnp.float32,
    )


def iotas(rows, cols):
    return (
        lax.broadcasted_iota(jnp.int32, (rows, cols), 0),
        lax.broadcasted_iota(jnp.int32, (rows, cols), 1),
    )


def eye(rows, cols):
    row, col = iotas(rows, cols)
    return (row == col).astype(jnp.float32)


def signed_half(plus, minus):
    return (0.5 * plus.astype(jnp.float32) - 0.5 * minus.astype(jnp.float32)).astype(jnp.bfloat16)


def eliminate(mats, sides):
    n = mats[0].shape[0]
    batch = len(mats)
    tiles = n // 8
    width = 2 * n
    work = [
        [jnp.concatenate([m, s], axis=1)[8 * i : 8 * i + 8] for i in range(tiles)]
        for m, s in zip(mats, sides)
    ]
    sub = lax.broadcasted_iota(jnp.int32, (8, width), 0)
    done = [[None] * tiles for _ in range(batch)]
    for p in range(tiles):
        cols = [
            [
                [
                    jnp.broadcast_to(work[b][i][:, 8 * p + k : 8 * p + k + 1], (8, width))
                    for i in range(p, tiles)
                ]
                for k in range(8)
            ]
            for b in range(batch)
        ]
        for b in range(batch):
            head = work[b][p]
            rest = [work[b][i] for i in range(p + 1, tiles)]
            scales = jnp.zeros((8, width), jnp.float32)
            for k in range(8):
                pivot = cols[b][k][0][k : k + 1]
                inv = 1.0 / pivot
                scales = jnp.where(sub == k, jnp.broadcast_to(inv, (8, width)), scales)
                row = head[k : k + 1] * inv
                across = [cols[b][j][0][k : k + 1] * inv for j in range(k + 1, 8)]
                below = jnp.where(sub > k, cols[b][k][0], 0.0)
                head = head - below * row
                for j in range(k + 1, 8):
                    cols[b][j][0] = cols[b][j][0] - below * across[j - k - 1]
                for i in range(1, tiles - p):
                    factor = cols[b][k][i]
                    rest[i - 1] = rest[i - 1] - factor * row
                    for j in range(k + 1, 8):
                        cols[b][j][i] = cols[b][j][i] - factor * across[j - k - 1]
            done[b][p] = head * jnp.sqrt(scales)
            for i in range(p + 1, tiles):
                work[b][i] = rest[i - p - 1]
    return [jnp.concatenate(done[b], axis=0)[:, n:] for b in range(batch)]


def total(entries):
    return jnp.sum(jnp.sum(entries, axis=0, keepdims=True), axis=1, keepdims=True)


def first_level(grams, first):
    width = first.shape[0]
    ident = eye(width, width)
    images = [mm(first, g, (0, 0)) for g in grams]
    reduced = [mm(z, first) for z in images]
    solved = eliminate(reduced, images)
    return [c * lax.rsqrt(total(g * ident) / width) for c, g in zip(solved, grams)]


def prepare(coefs, turn):
    width = turn.shape[0]
    lean = [mm(c, turn[:, i * width : (i + 1) * width], (0, 1)) for i, c in enumerate(coefs)]
    return jnp.concatenate(lean, axis=0), [mm(c, c, (0, 0)) for c in coefs]


def middle_level(pairs, ready):
    width = pairs[0].shape[0] // 2
    reduced, sides, scales = [], [], []
    for gram, (lean, norms) in zip(pairs, ready):
        image = mm(lean, gram, (0, 0))
        reduced.append(mm(image, lean))
        sides.append(
            jnp.concatenate([mm(image[:, :width], norms[0]), mm(image[:, width:], norms[1])], axis=1)
        )
        trace = total(norms[0] * gram[:width, :width]) + total(norms[1] * gram[width:, width:])
        scales.append(lax.rsqrt(trace / (2 * width)))
    inverses = eliminate(reduced, [eye(width, width)] * len(pairs))
    return [mm(inv, s) * k for inv, s, k in zip(inverses, sides, scales)]


def last_level(pairs, cross, weights, turn):
    width = turn.shape[0]
    lean = [mm(weights[u], turn[:, u * width : (u + 1) * width], (0, 1)) for u in (0, 1)]
    image = [mm(lean[u], pairs[u], (0, 0)) for u in (0, 1)]
    norms = [mm(weights[u], weights[u], (0, 0)) for u in (0, 1)]
    up = mm(lean[1], cross, (0, 0))
    down = mm(lean[0], cross, (0, 1))
    mixed = mm(up, lean[0])
    reduced = mm(image[0], lean[0]) + mm(image[1], lean[1]) + (mixed + mixed.T)
    trace = total(norms[0] * pairs[0]) + total(norms[1] * pairs[1])
    sides = jnp.concatenate([mm(image[0] + up, norms[0]), mm(image[1] + down, norms[1])], axis=1)
    inverse = eliminate([reduced], [eye(width, width)])[0]
    return mm(inverse, sides) * lax.rsqrt(trace / (2 * width))


def gather_kernel(
    quarter, nx, ny, nt,
    velocity_hbm, first_hbm, merge_hbm,
    coarse_ref, fine_ref, weight_ref,
    velocity, seeds_first, seeds_merge, chunk, edge_low, edge_high, column, rim_out,
    rims, land, column_in, halo_own, halo,
    own_coarse, own_fine, own_landed, shared, parts, landed, whole,
    load_sems, chunk_sems, column_sems, rim_sems, low_sems, high_sems,
    own_sems, own_in, share_sems, share_in, scatter_sems, scatter_in, spread_sems, spread_in,
):
    ix, iy, it = lax.axis_index("sx"), lax.axis_index("sy"), lax.axis_index("ta")
    plane = nx * ny
    devices = plane * nt
    place = ix * ny + iy
    me = it * plane + place
    rows3, lanes = chunk.shape[1:]
    snaps = rows3 // 3
    cells_x = lanes // quarter
    half3 = rows3 // 2
    partner = it + 1 - 2 * lax.rem(it, 2)
    near, far = lax.rem(it + 2, 4), 3 - it
    b16, f32 = jnp.bfloat16, jnp.float32

    def device(t):
        where = lax.rem(t, plane)
        return (lax.div(where, ny), lax.rem(where, ny), lax.div(t, plane))

    def copy(src, dst, send, recv, target):
        return pltpu.make_async_remote_copy(
            src_ref=src, dst_ref=dst, send_sem=send, recv_sem=recv, device_id=target, device_id_type=MESH
        )

    loads = [
        pltpu.make_async_copy(src, dst, load_sems.at[i])
        for i, (src, dst) in enumerate(
            ((velocity_hbm, velocity), (first_hbm, seeds_first), (merge_hbm, seeds_merge))
        )
    ]
    for c in loads:
        c.start()

    barrier = pltpu.get_barrier_semaphore()

    def greet(target):
        pl.semaphore_signal(barrier, inc=1, device_id=target, device_id_type=MESH)

    def greet_plane(j, carry):
        t = lax.rem(place + j, plane)
        greet((lax.div(t, ny), lax.rem(t, ny), it))
        return carry

    others = (partner, near, far)
    for t in others:
        greet((ix, iy, t))
    can_up, can_down = ix < nx - 1, ix > 0
    lax.fori_loop(1, plane, greet_plane, 0)
    expected = plane - 1 + 3

    right_ok, left_ok = iy + 1 < ny, iy > 0

    @pl.when(jnp.logical_not(can_down))
    def _():
        halo[:, :, :128] = jnp.zeros((3, half3, 128), b16)
        halo_own[:, :, :128] = jnp.zeros((nt, half3, 128), b16)

    @pl.when(jnp.logical_not(can_up))
    def _():
        halo[:, :, 128:] = jnp.zeros((3, half3, 128), b16)
        halo_own[:, :, 128:] = jnp.zeros((nt, half3, 128), b16)

    @pl.when(jnp.logical_not(left_ok))
    def _():
        rims[0] = jnp.zeros((16, rows3), b16)

    @pl.when(jnp.logical_not(right_ok))
    def _():
        rims[1] = jnp.zeros((16, rows3), b16)

    row, lane = iotas(16, lanes)
    pick_right = ((row < cells_x) & (lane == row * quarter + quarter - 1)).astype(f32).astype(b16)
    pick_left = (
        ((row >= cells_x) & (row < 2 * cells_x) & (lane == (row - cells_x) * quarter))
        .astype(f32)
        .astype(b16)
    )

    loads[0].wait()
    for c in range(3):
        field = velocity[c].astype(f32)
        rows = [field[:, x, :] for x in range(cells_x)]
        for q in range(nt):
            cut = slice(q * quarter, (q + 1) * quarter)
            piece = jnp.concatenate([r[:, cut] for r in rows], axis=1)
            chunk[q, c * snaps : (c + 1) * snaps] = piece.astype(b16)
    for q in range(nt):
        whole_piece = chunk[q].astype(f32)
        first_row = whole_piece[:, :quarter]
        last_row = whole_piece[:, lanes - quarter :]
        edge_low[q] = jnp.concatenate([first_row[:half3], first_row[half3:]], axis=1).astype(b16)
        edge_high[q] = jnp.concatenate([last_row[:half3], last_row[half3:]], axis=1).astype(b16)
    right_of = [dot16(pick_right, chunk[q], (1, 1)) for q in range(nt)]
    left_of = [dot16(pick_left, chunk[q], (1, 1)) for q in range(nt)]
    rim_out[0] = right_of[nt - 1].astype(b16)
    rim_out[1] = left_of[0].astype(b16)
    for q in (1, 2):
        column[q] = (right_of[q - 1] + left_of[q + 1]).astype(b16)

    pl.semaphore_wait(barrier, expected)

    def chunk_copy(i):
        t = others[i]
        return copy(chunk.at[t], land.at[i], chunk_sems.at[0, i], chunk_sems.at[1, i], (ix, iy, t))

    def column_copy(i):
        t = others[i]
        return copy(column.at[t], column_in.at[i], column_sems.at[0, i], column_sems.at[1, i], (ix, iy, t))

    def edge_copy(source, side, sems, to_x, i):
        at = pl.ds(128 * side, 128)
        if i < 3:
            t = others[i]
            return copy(halo_own.at[t, :, at], halo.at[i, :, at], sems.at[0, i], sems.at[1, i], (ix, iy, t))
        return copy(source, halo_own.at[:, :, at], sems.at[0, i], sems.at[1, i], (to_x, iy, it))

    def rim_copies():
        return (
            (right_ok, copy(rim_out.at[0], rims.at[0], rim_sems.at[0, 0], rim_sems.at[1, 0], (ix, jnp.minimum(iy + 1, ny - 1), it))),
            (left_ok, copy(rim_out.at[1], rims.at[1], rim_sems.at[0, 1], rim_sems.at[1, 1], (ix, jnp.maximum(iy - 1, 0), it))),
        )

    def high(i):
        return edge_copy(edge_high, 0, high_sems, jnp.minimum(ix + 1, nx - 1), i)

    def low(i):
        return edge_copy(edge_low, 1, low_sems, jnp.maximum(ix - 1, 0), i)

    def edges(i, act):
        if i == 3:
            pl.when(can_up)(lambda: act(high(i)))
            pl.when(can_down)(lambda: act(low(i)))
        else:
            pl.when(can_down)(lambda: act(high(i)))
            pl.when(can_up)(lambda: act(low(i)))

    def start(c):
        c.start()

    for ok, c in rim_copies():
        pl.when(ok)(functools.partial(start, c))
    edges(3, start)
    for i in (1, 2, 0):
        chunk_copy(i).start()
    def halo_wait(i):
        pl.when(can_down)(lambda: high(i).wait_recv())
        pl.when(can_up)(lambda: low(i).wait_recv())

    pl.when(left_ok)(lambda: rim_copies()[0][1].wait_recv())
    pl.when(right_ok)(lambda: rim_copies()[1][1].wait_recv())
    column[0] = (rims[0].astype(f32) + left_of[1]).astype(b16)
    column[nt - 1] = (right_of[nt - 2] + rims[1].astype(f32)).astype(b16)
    for i in (2, 1, 0):
        column_copy(i).start()
    halo_wait(3)
    for i in (2, 1, 0):
        edges(i, start)

    row, lane = iotas(lanes, lanes)
    gap = row - lane
    same = row // quarter == lane // quarter
    both = jnp.concatenate(
        [
            signed_half(gap == quarter, gap == -quarter),
            signed_half((gap == 1) & same, (gap == -1) & same),
        ],
        axis=1,
    )
    row, lane = iotas(256, 2 * lanes)
    wide, at = lane // lanes, lax.rem(lane, lanes)
    rise, k = row // 128, lax.rem(row, 128)
    hit = k // quarter == wide
    k = lax.rem(k, quarter)
    outer = signed_half(
        hit & (rise == 1) & (at == k + lanes - quarter), hit & (rise == 0) & (at == k)
    )
    row, lane = iotas(16, lanes)
    rim = signed_half(
        (row >= cells_x) & (row < 2 * cells_x) & (lane == (row - cells_x) * quarter + quarter - 1),
        (row < cells_x) & (lane == row * quarter),
    )

    def strain(block, border, sides):
        inner = dot16(block, both)
        across = dot16(border, outer)
        dx = inner[:, :lanes] + jnp.concatenate([across[:, :lanes], across[:, lanes:]], axis=0)
        dy = inner[:, lanes:] + dot16(sides, rim, (0, 0))
        ux, vx, wx = (dx[i * snaps : (i + 1) * snaps] for i in range(3))
        uy, vy, wy = (dy[i * snaps : (i + 1) * snaps] for i in range(3))
        fields = jnp.concatenate([ux, vy, 0.5 * (uy + vx), 0.5 * wx, 0.5 * wy], axis=1)
        coarse = fields.astype(b16)
        return coarse, (fields - coarse.astype(f32)).astype(b16)

    def keep(block, values):
        at = pl.ds(pl.multiple_of(block * snaps, snaps), snaps)
        coarse_ref[at], fine_ref[at] = values

    own = jnp.zeros((snaps, 2 * snaps), f32)
    for q in range(nt):
        coarse, fine = strain(chunk[q], halo_own[q], column[q])
        own_coarse[q], own_fine[q] = coarse, fine
        own = own + dot16(coarse, jnp.concatenate([coarse, fine], axis=0), (1, 1))
    skew = own[:, snaps:]
    own = own[:, :snaps] + (skew + skew.T)
    half = snaps // 2
    own_landed[place] = jnp.concatenate([own[:half], own[half:]], axis=1)

    def own_copies(act):
        def body(j, carry):
            t = lax.rem(place + j, plane)
            act(
                copy(
                    own_landed.at[place], own_landed.at[place], own_sems.at[j], own_in.at[0],
                    (lax.div(t, ny), lax.rem(t, ny), it),
                )
            )
            return carry

        lax.fori_loop(1, plane, body, 0)

    own_copies(start)
    keep(it, (own_coarse[it], own_fine[it]))
    for i in range(3):
        chunk_copy(i).wait_recv()
        halo_wait(i)
        column_copy(i).wait_recv()
        keep(others[i], strain(land[i], halo[i], column_in[i]))
    pair = 2 * snaps

    def gram(high, low):
        coarse, fine = coarse_ref[low], fine_ref[low]
        size = coarse.shape[0]
        both_low = dot16(coarse_ref[high], jnp.concatenate([coarse, fine], axis=0), (1, 1))
        return both_low[:, :size] + (both_low[:, size:] + dot16(fine_ref[high], coarse, (1, 1)))

    rank = jnp.where(it == 0, 2, jnp.where(it == 3, 3, it - 1)) * plane + place
    owner = rank < OWNERS
    slot = jnp.minimum(rank, OWNERS - 1)

    def scatter(first_piece, last_piece, act):
        for j in range(first_piece, last_piece):
            if j < LEAD:
                k = lax.rem(place + j, LEAD)
            else:
                k = LEAD + lax.rem(place + j, OWNERS - LEAD)
            group, where = lax.div(k, plane), lax.rem(k, plane)
            level = jnp.where(group == 2, 0, jnp.where(group == 3, 3, group + 1))
            c = copy(
                parts.at[k], landed.at[rank], scatter_sems.at[j], scatter_in.at[0],
                (lax.div(where, ny), lax.rem(where, ny), level),
            )
            pl.when(rank != k)(functools.partial(act, c))

    lead = slot < LEAD

    def spread(act):
        def body(t, carry):
            c = copy(
                whole.at[slot], whole.at[slot], spread_sems.at[t], spread_in.at[jnp.where(lead, 0, 1)],
                device(t),
            )
            pl.when(t != me)(functools.partial(act, c))
            return carry

        @pl.when(owner)
        def _():
            lax.fori_loop(0, devices, body, 0)

    blocks = [slice(b * snaps, (b + 1) * snaps) for b in range(nt)]
    mixed = jnp.concatenate([gram(blocks[1], blocks[0]), gram(blocks[3], blocks[2])], axis=1)
    parts[:LEAD] = mixed.reshape(LEAD, 8, pair)
    scatter(0, LEAD, start)
    parts[LEAD:] = gram(slice(pair, 2 * pair), slice(0, pair)).reshape(OWNERS - LEAD, 8, pair)
    scatter(LEAD, OWNERS, start)

    for c in loads[1:]:
        c.wait()
    first = eye(snaps, snaps) + seeds_first[...].astype(f32) * (0.5 / 512.0)
    stacked = jnp.concatenate([eye(snaps, snaps)] * 2, axis=1) * (2.0**-0.5)
    turns = [
        stacked + seeds_merge[level].astype(f32) * (0.5 / (64.0 * 128.0**0.5)) for level in range(2)
    ]
    some = own_landed.at[pl.ds(0, plane - 1)]
    copy(some, some, own_sems.at[0], own_in.at[0], (ix, iy, partner)).wait_recv()
    packed = jnp.sum(own_landed[...], axis=0)
    own = jnp.concatenate([packed[:, :snaps], packed[:, snaps:]], axis=0)
    shared[it] = jnp.concatenate([first_level([own], first)[0], own], axis=1)

    def share_copy(i):
        return copy(shared.at[it], shared.at[it], share_sems.at[i], share_in.at[0], (ix, iy, others[i]))

    for i in range(3):
        share_copy(i).start()

    @pl.when(owner)
    def _():
        landed[rank] = parts[slot]
        some = landed.at[pl.ds(0, devices - 1)]
        copy(some, some, scatter_sems.at[0], scatter_in.at[0], (ix, iy, partner)).wait_recv()
        whole[slot] = jnp.sum(landed[...], axis=0)

    spread(start)
    some = shared.at[pl.ds(0, nt - 1)]
    copy(some, some, share_sems.at[0], share_in.at[0], (ix, iy, partner)).wait_recv()
    coefs = [shared[b][:, :snaps] for b in range(nt)]
    grams = [shared[b][:, snaps:] for b in range(nt)]

    ready = [prepare(coefs[2 * u : 2 * u + 2], turns[0]) for u in range(2)]

    def arrived(part, first_piece, count, own_piece):
        def wait(pieces):
            some = whole.at[pl.ds(first_piece, pieces)]
            copy(some, some, spread_sems.at[0], spread_in.at[part], (ix, iy, partner)).wait_recv()

        pl.when(own_piece)(lambda: wait(count - 1))
        pl.when(jnp.logical_not(own_piece))(lambda: wait(count))
        return whole[first_piece : first_piece + count].reshape(count * 8, pair)

    rows = arrived(0, 0, LEAD, jnp.logical_and(owner, lead))
    pairs = []
    for u in range(2):
        mixed = rows[:, u * snaps : (u + 1) * snaps]
        pairs.append(
            jnp.concatenate(
                [
                    jnp.concatenate([grams[2 * u], mixed.T], axis=1),
                    jnp.concatenate([mixed, grams[2 * u + 1]], axis=1),
                ],
                axis=0,
            )
        )
    weights = middle_level(pairs, ready)
    cross = arrived(1, LEAD, OWNERS - LEAD, jnp.logical_and(owner, jnp.logical_not(lead)))
    weight_ref[...] = last_level(pairs, cross, weights, turns[1])

    def finish(c):
        c.wait_send()

    for ok, c in rim_copies():
        pl.when(ok)(functools.partial(finish, c))
    for i in range(3):
        finish(chunk_copy(i))
        finish(column_copy(i))
        finish(share_copy(i))
    for i in range(4):
        edges(i, finish)
    own_copies(finish)
    scatter(0, OWNERS, finish)
    spread(finish)


def tail_kernel(weight_ref, coarse_ref, fine_ref, out_hbm, out, sem):
    modes, lanes = weight_ref.shape[0], coarse_ref.shape[1]
    weights = weight_ref[...]
    coarse = weights.astype(jnp.bfloat16)
    fine = (weights - coarse.astype(jnp.float32)).astype(jnp.bfloat16)
    both = dot16(jnp.concatenate([coarse, fine], axis=0), coarse_ref[...])
    basis = both[:modes] + (both[modes:] + dot16(coarse, fine_ref[...]))
    quarter = out.shape[1]
    strips = lanes // quarter
    for i in range(strips):
        out[pl.ds(i, modes, stride=strips), :] = basis[:, i * quarter : (i + 1) * quarter]
    done = pltpu.make_async_copy(out, out_hbm, sem)
    done.start()
    done.wait()


def local(velocity, seeds_first, seeds_merge):
    comps, width, cells_x, cells_y = velocity.shape
    nx, ny, nt = (lax.axis_size(a) for a in ("sx", "sy", "ta"))
    quarter = cells_y // nt
    lanes = cells_x * quarter
    plane = nx * ny
    rows3 = comps * width
    pair = 2 * width
    vmem = pl.BlockSpec(memory_space=pltpu.VMEM)
    hbm = pl.BlockSpec(memory_space=pltpu.HBM)
    b16, f32 = jnp.bfloat16, jnp.float32
    dma = pltpu.SemaphoreType.DMA
    coarse, fine, weights = pl.pallas_call(
        functools.partial(gather_kernel, quarter, nx, ny, nt),
        out_shape=(
            jax.ShapeDtypeStruct((nt * width, 5 * lanes), b16),
            jax.ShapeDtypeStruct((nt * width, 5 * lanes), b16),
            jax.ShapeDtypeStruct((width, nt * width), f32),
        ),
        in_specs=[hbm] * 3,
        out_specs=(vmem,) * 3,
        scratch_shapes=[
            pltpu.VMEM(velocity.shape, b16),
            pltpu.VMEM((width, width), jnp.int32),
            pltpu.VMEM((2, width, pair), jnp.int32),
            pltpu.VMEM((nt, rows3, lanes), b16),
            pltpu.VMEM((nt, rows3 // 2, 128), b16),
            pltpu.VMEM((nt, rows3 // 2, 128), b16),
            pltpu.VMEM((nt, 16, rows3), b16),
            pltpu.VMEM((2, 16, rows3), b16),
            pltpu.VMEM((2, 16, rows3), b16),
            pltpu.VMEM((3, rows3, lanes), b16),
            pltpu.VMEM((3, 16, rows3), b16),
            pltpu.VMEM((nt, rows3 // 2, 256), b16),
            pltpu.VMEM((3, rows3 // 2, 256), b16),
            pltpu.VMEM((nt, width, 5 * lanes), b16),
            pltpu.VMEM((nt, width, 5 * lanes), b16),
            pltpu.VMEM((plane, width // 2, pair), f32),
            pltpu.VMEM((nt, width, pair), f32),
            pltpu.VMEM((OWNERS, 8, pair), f32),
            pltpu.VMEM((nt * plane, 8, pair), f32),
            pltpu.VMEM((OWNERS, 8, pair), f32),
            dma((3,)),
            dma((2, 3)),
            dma((2, 3)),
            dma((2, 2)),
            dma((2, 4)),
            dma((2, 4)),
            dma((plane,)),
            dma((1,)),
            dma((3,)),
            dma((1,)),
            dma((OWNERS,)),
            dma((1,)),
            dma((nt * plane,)),
            dma((2,)),
        ],
        compiler_params=pltpu.CompilerParams(
            collective_id=0, has_side_effects=True, vmem_limit_bytes=40 * 2**20
        ),
        name="gather",
    )(*(pltpu.with_memory_space_constraint(a, pltpu.HBM) for a in (velocity, seeds_first, seeds_merge.transpose(0, 2, 1))))
    strips = 5 * cells_x
    out = pl.pallas_call(
        tail_kernel,
        out_shape=jax.ShapeDtypeStruct((width * strips, quarter), f32),
        in_specs=[vmem] * 3,
        out_specs=hbm,
        scratch_shapes=[pltpu.VMEM((width * strips, quarter), f32), dma],
        compiler_params=pltpu.CompilerParams(vmem_limit_bytes=32 * 2**20),
        name="tail",
    )(weights, coarse, fine)
    return out.reshape(width, 5, cells_x, quarter)


def solution(mesh):
    in_specs = (P(None, "ta", "sx", "sy"), P(), P())
    out_specs = P(None, None, "sx", ("sy", "ta"))
    return jax.shard_map(local, mesh=mesh, in_specs=in_specs, out_specs=out_specs, check_vma=False)
```

```python
import functools

import jax
import jax.numpy as jnp
from jax import lax
from jax.experimental import pallas as pl
from jax.experimental.pallas import tpu as pltpu
from jax.sharding import PartitionSpec as P

HI = lax.Precision.HIGHEST
MESH = pl.DeviceIdType.MESH
OWNERS = 24
LEAD = 8


def mm(left, right, contract=(1, 0)):
    return lax.dot_general(
        left,
        right,
        (((contract[0],), (contract[1],)), ((), ())),
        precision=HI,
        preferred_element_type=jnp.float32,
    )


def dot16(left, right, contract=(1, 0)):
    return lax.dot_general(
        left,
        right,
        (((contract[0],), (contract[1],)), ((), ())),
        preferred_element_type=jnp.float32,
    )


def iotas(rows, cols):
    return (
        lax.broadcasted_iota(jnp.int32, (rows, cols), 0),
        lax.broadcasted_iota(jnp.int32, (rows, cols), 1),
    )


def eye(rows, cols):
    row, col = iotas(rows, cols)
    return (row == col).astype(jnp.float32)


def signed_half(plus, minus):
    return (0.5 * plus.astype(jnp.float32) - 0.5 * minus.astype(jnp.float32)).astype(jnp.bfloat16)


def eliminate(mats, sides):
    n = mats[0].shape[0]
    batch = len(mats)
    tiles = n // 8
    width = 2 * n
    work = [
        [jnp.concatenate([m, s], axis=1)[8 * i : 8 * i + 8] for i in range(tiles)]
        for m, s in zip(mats, sides)
    ]
    sub = lax.broadcasted_iota(jnp.int32, (8, width), 0)
    done = [[None] * tiles for _ in range(batch)]
    for p in range(tiles):
        cols = [
            [
                [
                    jnp.broadcast_to(work[b][i][:, 8 * p + k : 8 * p + k + 1], (8, width))
                    for i in range(p, tiles)
                ]
                for k in range(8)
            ]
            for b in range(batch)
        ]
        for b in range(batch):
            head = work[b][p]
            rest = [work[b][i] for i in range(p + 1, tiles)]
            scales = jnp.zeros((8, width), jnp.float32)
            for k in range(8):
                pivot = cols[b][k][0][k : k + 1]
                inv = 1.0 / pivot
                scales = jnp.where(sub == k, jnp.broadcast_to(inv, (8, width)), scales)
                row = head[k : k + 1] * inv
                across = [cols[b][j][0][k : k + 1] * inv for j in range(k + 1, 8)]
                below = jnp.where(sub > k, cols[b][k][0], 0.0)
                head = head - below * row
                for j in range(k + 1, 8):
                    cols[b][j][0] = cols[b][j][0] - below * across[j - k - 1]
                for i in range(1, tiles - p):
                    factor = cols[b][k][i]
                    rest[i - 1] = rest[i - 1] - factor * row
                    for j in range(k + 1, 8):
                        cols[b][j][i] = cols[b][j][i] - factor * across[j - k - 1]
            done[b][p] = head * jnp.sqrt(scales)
            for i in range(p + 1, tiles):
                work[b][i] = rest[i - p - 1]
    return [jnp.concatenate(done[b], axis=0)[:, n:] for b in range(batch)]


def total(entries):
    return jnp.sum(jnp.sum(entries, axis=0, keepdims=True), axis=1, keepdims=True)


def first_level(grams, first):
    width = first.shape[0]
    ident = eye(width, width)
    images = [mm(first, g, (0, 0)) for g in grams]
    reduced = [mm(z, first) for z in images]
    solved = eliminate(reduced, images)
    return [c * lax.rsqrt(total(g * ident) / width) for c, g in zip(solved, grams)]


def prepare(coefs, turn):
    width = turn.shape[0]
    lean = [mm(c, turn[:, i * width : (i + 1) * width], (0, 1)) for i, c in enumerate(coefs)]
    return jnp.concatenate(lean, axis=0), [mm(c, c, (0, 0)) for c in coefs]


def middle_level(pairs, ready):
    width = pairs[0].shape[0] // 2
    reduced, sides, scales = [], [], []
    for gram, (lean, norms) in zip(pairs, ready):
        image = mm(lean, gram, (0, 0))
        reduced.append(mm(image, lean))
        sides.append(
            jnp.concatenate([mm(image[:, :width], norms[0]), mm(image[:, width:], norms[1])], axis=1)
        )
        trace = total(norms[0] * gram[:width, :width]) + total(norms[1] * gram[width:, width:])
        scales.append(lax.rsqrt(trace / (2 * width)))
    inverses = eliminate(reduced, [eye(width, width)] * len(pairs))
    return [mm(inv, s) * k for inv, s, k in zip(inverses, sides, scales)]


def last_level(pairs, cross, weights, turn):
    width = turn.shape[0]
    lean = [mm(weights[u], turn[:, u * width : (u + 1) * width], (0, 1)) for u in (0, 1)]
    image = [mm(lean[u], pairs[u], (0, 0)) for u in (0, 1)]
    norms = [mm(weights[u], weights[u], (0, 0)) for u in (0, 1)]
    up = mm(lean[1], cross, (0, 0))
    down = mm(lean[0], cross, (0, 1))
    mixed = mm(up, lean[0])
    reduced = mm(image[0], lean[0]) + mm(image[1], lean[1]) + (mixed + mixed.T)
    trace = total(norms[0] * pairs[0]) + total(norms[1] * pairs[1])
    sides = jnp.concatenate([mm(image[0] + up, norms[0]), mm(image[1] + down, norms[1])], axis=1)
    inverse = eliminate([reduced], [eye(width, width)])[0]
    return mm(inverse, sides) * lax.rsqrt(trace / (2 * width))


def gather_kernel(
    quarter, nx, ny, nt,
    velocity_hbm, first_hbm, merge_hbm,
    coarse_ref, fine_ref, weight_ref,
    velocity, seeds_first, seeds_merge, chunk, edge_low, edge_high, column, rim_out,
    rims, land, column_in, halo_own, halo, passed,
    own_coarse, own_fine, own_landed, shared, parts, landed, whole,
    load_sems, chunk_sems, column_sems, rim_sems, low_sems, high_sems,
    own_sems, own_in, share_sems, share_in, scatter_sems, scatter_in, spread_sems, spread_in,
):
    ix, iy, it = lax.axis_index("sx"), lax.axis_index("sy"), lax.axis_index("ta")
    plane = nx * ny
    devices = plane * nt
    place = ix * ny + iy
    me = it * plane + place
    rows3, lanes = chunk.shape[1:]
    snaps = rows3 // 3
    cells_x = lanes // quarter
    half3 = rows3 // 2
    partner = it + 1 - 2 * lax.rem(it, 2)
    near, far = lax.rem(it + 2, 4), 3 - it
    b16, f32 = jnp.bfloat16, jnp.float32

    def device(t):
        where = lax.rem(t, plane)
        return (lax.div(where, ny), lax.rem(where, ny), lax.div(t, plane))

    def copy(src, dst, send, recv, target):
        return pltpu.make_async_remote_copy(
            src_ref=src, dst_ref=dst, send_sem=send, recv_sem=recv, device_id=target, device_id_type=MESH
        )

    loads = [
        pltpu.make_async_copy(src, dst, load_sems.at[i])
        for i, (src, dst) in enumerate(
            ((velocity_hbm, velocity), (first_hbm, seeds_first), (merge_hbm, seeds_merge))
        )
    ]
    for c in loads:
        c.start()

    barrier = pltpu.get_barrier_semaphore()

    def greet(target):
        pl.semaphore_signal(barrier, inc=1, device_id=target, device_id_type=MESH)

    def greet_plane(j, carry):
        t = lax.rem(place + j, plane)
        greet((lax.div(t, ny), lax.rem(t, ny), it))
        return carry

    others = (partner, near, far)
    for t in others:
        greet((ix, iy, t))
    can_up, can_down = ix < nx - 1, ix > 0
    lax.fori_loop(1, plane, greet_plane, 0)
    expected = plane - 1 + 3

    right_ok, left_ok = iy + 1 < ny, iy > 0

    @pl.when(jnp.logical_not(can_down))
    def _():
        halo[:, :, :128] = jnp.zeros((3, half3, 128), b16)
        halo_own[:, :, :128] = jnp.zeros((nt, half3, 128), b16)
        passed[0] = jnp.zeros((rows3, 128), b16)

    @pl.when(jnp.logical_not(can_up))
    def _():
        halo[:, :, 128:] = jnp.zeros((3, half3, 128), b16)
        halo_own[:, :, 128:] = jnp.zeros((nt, half3, 128), b16)
        passed[1] = jnp.zeros((rows3, 128), b16)

    @pl.when(jnp.logical_not(left_ok))
    def _():
        rims[0] = jnp.zeros((16, rows3), b16)

    @pl.when(jnp.logical_not(right_ok))
    def _():
        rims[1] = jnp.zeros((16, rows3), b16)

    row, lane = iotas(16, lanes)
    pick_right = ((row < cells_x) & (lane == row * quarter + quarter - 1)).astype(f32).astype(b16)
    pick_left = (
        ((row >= cells_x) & (row < 2 * cells_x) & (lane == (row - cells_x) * quarter))
        .astype(f32)
        .astype(b16)
    )

    loads[0].wait()
    for c in range(3):
        field = velocity[c].astype(f32)
        rows = [field[:, x, :] for x in range(cells_x)]
        for q in range(nt):
            cut = slice(q * quarter, (q + 1) * quarter)
            piece = jnp.concatenate([r[:, cut] for r in rows], axis=1)
            chunk[q, c * snaps : (c + 1) * snaps] = piece.astype(b16)
    for q in range(nt):
        whole_piece = chunk[q].astype(f32)
        first_row = whole_piece[:, :quarter]
        last_row = whole_piece[:, lanes - quarter :]
        edge_low[q] = jnp.concatenate([first_row[:half3], first_row[half3:]], axis=1).astype(b16)
        edge_high[q] = jnp.concatenate([last_row[:half3], last_row[half3:]], axis=1).astype(b16)
    right_of = [dot16(pick_right, chunk[q], (1, 1)) for q in range(nt)]
    left_of = [dot16(pick_left, chunk[q], (1, 1)) for q in range(nt)]
    rim_out[0] = right_of[nt - 1].astype(b16)
    rim_out[1] = left_of[0].astype(b16)
    for q in (1, 2):
        column[q] = (right_of[q - 1] + left_of[q + 1]).astype(b16)

    pl.semaphore_wait(barrier, expected)

    def chunk_copy(i):
        t = others[i]
        return copy(chunk.at[t], land.at[i], chunk_sems.at[0, i], chunk_sems.at[1, i], (ix, iy, t))

    def column_copy(i):
        t = others[i]
        return copy(column.at[t], column_in.at[i], column_sems.at[0, i], column_sems.at[1, i], (ix, iy, t))

    def edge_copy(source, side, sems, to_x, i):
        at = pl.ds(128 * side, 128)
        if i == 1:
            src = land.at[1, :, pl.ds((1 - side) * (lanes - 128), 128)]
            return copy(src, passed.at[side], sems.at[0, i], sems.at[1, i], (to_x, iy, it))
        if i < 3:
            t = others[i]
            return copy(halo_own.at[t, :, at], halo.at[i, :, at], sems.at[0, i], sems.at[1, i], (ix, iy, t))
        return copy(source, halo_own.at[:, :, at], sems.at[0, i], sems.at[1, i], (to_x, iy, it))

    def rim_copies():
        return (
            (right_ok, copy(rim_out.at[0], rims.at[0], rim_sems.at[0, 0], rim_sems.at[1, 0], (ix, jnp.minimum(iy + 1, ny - 1), it))),
            (left_ok, copy(rim_out.at[1], rims.at[1], rim_sems.at[0, 1], rim_sems.at[1, 1], (ix, jnp.maximum(iy - 1, 0), it))),
        )

    def high(i):
        return edge_copy(edge_high, 0, high_sems, jnp.minimum(ix + 1, nx - 1), i)

    def low(i):
        return edge_copy(edge_low, 1, low_sems, jnp.maximum(ix - 1, 0), i)

    def edges(i, act):
        if i in (1, 3):
            pl.when(can_up)(lambda: act(high(i)))
            pl.when(can_down)(lambda: act(low(i)))
        else:
            pl.when(can_down)(lambda: act(high(i)))
            pl.when(can_up)(lambda: act(low(i)))

    def start(c):
        c.start()

    for ok, c in rim_copies():
        pl.when(ok)(functools.partial(start, c))
    edges(3, start)
    for i in (1, 0, 2):
        chunk_copy(i).start()
    def halo_wait(i):
        pl.when(can_down)(lambda: high(i).wait_recv())
        pl.when(can_up)(lambda: low(i).wait_recv())

    pl.when(left_ok)(lambda: rim_copies()[0][1].wait_recv())
    pl.when(right_ok)(lambda: rim_copies()[1][1].wait_recv())
    column[0] = (rims[0].astype(f32) + left_of[1]).astype(b16)
    column[nt - 1] = (right_of[nt - 2] + rims[1].astype(f32)).astype(b16)
    for i in (2, 1, 0):
        column_copy(i).start()
    halo_wait(3)
    for i in (2, 0):
        edges(i, start)

    row, lane = iotas(lanes, lanes)
    gap = row - lane
    same = row // quarter == lane // quarter
    both = jnp.concatenate(
        [
            signed_half(gap == quarter, gap == -quarter),
            signed_half((gap == 1) & same, (gap == -1) & same),
        ],
        axis=1,
    )
    row, lane = iotas(256, 2 * lanes)
    wide, at = lane // lanes, lax.rem(lane, lanes)
    rise, k = row // 128, lax.rem(row, 128)
    hit = k // quarter == wide
    k = lax.rem(k, quarter)
    outer = signed_half(
        hit & (rise == 1) & (at == k + lanes - quarter), hit & (rise == 0) & (at == k)
    )
    row, lane = iotas(16, lanes)
    rim = signed_half(
        (row >= cells_x) & (row < 2 * cells_x) & (lane == (row - cells_x) * quarter + quarter - 1),
        (row < cells_x) & (lane == row * quarter),
    )

    row, lane = iotas(256, lanes)
    k = lax.rem(row, 128)
    beside = signed_half(
        (row >= 128) & (k < quarter) & (lane == k + lanes - quarter),
        (row < 128) & (lane == k - (128 - quarter)),
    )

    def strain(block, border, sides):
        inner = dot16(block, both)
        if border is None:
            across = dot16(jnp.concatenate([passed[0], passed[1]], axis=1), beside)
        else:
            across = dot16(border, outer)
            across = jnp.concatenate([across[:, :lanes], across[:, lanes:]], axis=0)
        dx = inner[:, :lanes] + across
        dy = inner[:, lanes:] + dot16(sides, rim, (0, 0))
        ux, vx, wx = (dx[i * snaps : (i + 1) * snaps] for i in range(3))
        uy, vy, wy = (dy[i * snaps : (i + 1) * snaps] for i in range(3))
        fields = jnp.concatenate([ux, vy, 0.5 * (uy + vx), 0.5 * wx, 0.5 * wy], axis=1)
        coarse = fields.astype(b16)
        return coarse, (fields - coarse.astype(f32)).astype(b16)

    def keep(block, values):
        at = pl.ds(pl.multiple_of(block * snaps, snaps), snaps)
        coarse_ref[at], fine_ref[at] = values

    own = jnp.zeros((snaps, 2 * snaps), f32)
    for q in range(nt):
        coarse, fine = strain(chunk[q], halo_own[q], column[q])
        own_coarse[q], own_fine[q] = coarse, fine
        own = own + dot16(coarse, jnp.concatenate([coarse, fine], axis=0), (1, 1))
    skew = own[:, snaps:]
    own = own[:, :snaps] + (skew + skew.T)
    half = snaps // 2
    own_landed[place] = jnp.concatenate([own[:half], own[half:]], axis=1)

    def own_copies(act):
        def body(j, carry):
            t = lax.rem(place + j, plane)
            act(
                copy(
                    own_landed.at[place], own_landed.at[place], own_sems.at[j], own_in.at[0],
                    (lax.div(t, ny), lax.rem(t, ny), it),
                )
            )
            return carry

        lax.fori_loop(1, plane, body, 0)

    own_copies(start)
    keep(it, (own_coarse[it], own_fine[it]))
    chunk_copy(1).wait_recv()
    edges(1, start)
    for i in (0, 2, 1):
        if i != 1:
            chunk_copy(i).wait_recv()
        halo_wait(i)
        column_copy(i).wait_recv()
        keep(others[i], strain(land[i], None if i == 1 else halo[i], column_in[i]))
    pair = 2 * snaps

    def gram(high, low):
        coarse, fine = coarse_ref[low], fine_ref[low]
        size = coarse.shape[0]
        both_low = dot16(coarse_ref[high], jnp.concatenate([coarse, fine], axis=0), (1, 1))
        return both_low[:, :size] + (both_low[:, size:] + dot16(fine_ref[high], coarse, (1, 1)))

    rank = jnp.where(it == 0, 2, jnp.where(it == 3, 3, it - 1)) * plane + place
    owner = rank < OWNERS
    slot = jnp.minimum(rank, OWNERS - 1)

    def scatter(first_piece, last_piece, act):
        for j in range(first_piece, last_piece):
            if j < LEAD:
                k = lax.rem(place + j, LEAD)
            else:
                k = LEAD + lax.rem(place + j, OWNERS - LEAD)
            group, where = lax.div(k, plane), lax.rem(k, plane)
            level = jnp.where(group == 2, 0, jnp.where(group == 3, 3, group + 1))
            c = copy(
                parts.at[k], landed.at[rank], scatter_sems.at[j], scatter_in.at[0],
                (lax.div(where, ny), lax.rem(where, ny), level),
            )
            pl.when(rank != k)(functools.partial(act, c))

    lead = slot < LEAD

    def spread(act):
        def body(t, carry):
            c = copy(
                whole.at[slot], whole.at[slot], spread_sems.at[t], spread_in.at[jnp.where(lead, 0, 1)],
                device(t),
            )
            pl.when(t != me)(functools.partial(act, c))
            return carry

        @pl.when(owner)
        def _():
            lax.fori_loop(0, devices, body, 0)

    blocks = [slice(b * snaps, (b + 1) * snaps) for b in range(nt)]
    mixed = jnp.concatenate([gram(blocks[1], blocks[0]), gram(blocks[3], blocks[2])], axis=1)
    parts[:LEAD] = mixed.reshape(LEAD, 8, pair)
    scatter(0, LEAD, start)
    parts[LEAD:] = gram(slice(pair, 2 * pair), slice(0, pair)).reshape(OWNERS - LEAD, 8, pair)
    scatter(LEAD, OWNERS, start)

    for c in loads[1:]:
        c.wait()
    first = eye(snaps, snaps) + seeds_first[...].astype(f32) * (0.5 / 512.0)
    stacked = jnp.concatenate([eye(snaps, snaps)] * 2, axis=1) * (2.0**-0.5)
    turns = [
        stacked + seeds_merge[level].astype(f32) * (0.5 / (64.0 * 128.0**0.5)) for level in range(2)
    ]
    some = own_landed.at[pl.ds(0, plane - 1)]
    copy(some, some, own_sems.at[0], own_in.at[0], (ix, iy, partner)).wait_recv()
    packed = jnp.sum(own_landed[...], axis=0)
    own = jnp.concatenate([packed[:, :snaps], packed[:, snaps:]], axis=0)
    shared[it] = jnp.concatenate([first_level([own], first)[0], own], axis=1)

    def share_copy(i):
        return copy(shared.at[it], shared.at[it], share_sems.at[i], share_in.at[0], (ix, iy, others[i]))

    for i in range(3):
        share_copy(i).start()

    @pl.when(owner)
    def _():
        landed[rank] = parts[slot]
        some = landed.at[pl.ds(0, devices - 1)]
        copy(some, some, scatter_sems.at[0], scatter_in.at[0], (ix, iy, partner)).wait_recv()
        whole[slot] = jnp.sum(landed[...], axis=0)

    spread(start)
    some = shared.at[pl.ds(0, nt - 1)]
    copy(some, some, share_sems.at[0], share_in.at[0], (ix, iy, partner)).wait_recv()
    coefs = [shared[b][:, :snaps] for b in range(nt)]
    grams = [shared[b][:, snaps:] for b in range(nt)]

    ready = [prepare(coefs[2 * u : 2 * u + 2], turns[0]) for u in range(2)]

    def arrived(part, first_piece, count, own_piece):
        def wait(pieces):
            some = whole.at[pl.ds(first_piece, pieces)]
            copy(some, some, spread_sems.at[0], spread_in.at[part], (ix, iy, partner)).wait_recv()

        pl.when(own_piece)(lambda: wait(count - 1))
        pl.when(jnp.logical_not(own_piece))(lambda: wait(count))
        return whole[first_piece : first_piece + count].reshape(count * 8, pair)

    def finish(c):
        c.wait_send()

    for ok, c in rim_copies():
        pl.when(ok)(functools.partial(finish, c))
    for i in range(3):
        finish(chunk_copy(i))
        finish(column_copy(i))
        finish(share_copy(i))
    for i in range(4):
        edges(i, finish)
    own_copies(finish)
    scatter(0, OWNERS, finish)
    spread(finish)

    rows = arrived(0, 0, LEAD, jnp.logical_and(owner, lead))
    pairs = []
    for u in range(2):
        mixed = rows[:, u * snaps : (u + 1) * snaps]
        pairs.append(
            jnp.concatenate(
                [
                    jnp.concatenate([grams[2 * u], mixed.T], axis=1),
                    jnp.concatenate([mixed, grams[2 * u + 1]], axis=1),
                ],
                axis=0,
            )
        )
    weights = middle_level(pairs, ready)
    cross = arrived(1, LEAD, OWNERS - LEAD, jnp.logical_and(owner, jnp.logical_not(lead)))
    weight_ref[...] = last_level(pairs, cross, weights, turns[1])


def tail_kernel(weight_ref, coarse_ref, fine_ref, out_hbm, out, sem):
    modes, lanes = weight_ref.shape[0], coarse_ref.shape[1]
    weights = weight_ref[...]
    coarse = weights.astype(jnp.bfloat16)
    fine = (weights - coarse.astype(jnp.float32)).astype(jnp.bfloat16)
    both = dot16(jnp.concatenate([coarse, fine], axis=0), coarse_ref[...])
    basis = both[:modes] + (both[modes:] + dot16(coarse, fine_ref[...]))
    quarter = out.shape[1]
    strips = lanes // quarter
    for i in range(strips):
        out[pl.ds(i, modes, stride=strips), :] = basis[:, i * quarter : (i + 1) * quarter]
    done = pltpu.make_async_copy(out, out_hbm, sem)
    done.start()
    done.wait()


def local(velocity, seeds_first, seeds_merge):
    comps, width, cells_x, cells_y = velocity.shape
    nx, ny, nt = (lax.axis_size(a) for a in ("sx", "sy", "ta"))
    quarter = cells_y // nt
    lanes = cells_x * quarter
    plane = nx * ny
    rows3 = comps * width
    pair = 2 * width
    vmem = pl.BlockSpec(memory_space=pltpu.VMEM)
    hbm = pl.BlockSpec(memory_space=pltpu.HBM)
    b16, f32 = jnp.bfloat16, jnp.float32
    dma = pltpu.SemaphoreType.DMA
    coarse, fine, weights = pl.pallas_call(
        functools.partial(gather_kernel, quarter, nx, ny, nt),
        out_shape=(
            jax.ShapeDtypeStruct((nt * width, 5 * lanes), b16),
            jax.ShapeDtypeStruct((nt * width, 5 * lanes), b16),
            jax.ShapeDtypeStruct((width, nt * width), f32),
        ),
        in_specs=[hbm] * 3,
        out_specs=(vmem,) * 3,
        scratch_shapes=[
            pltpu.VMEM(velocity.shape, b16),
            pltpu.VMEM((width, width), jnp.int32),
            pltpu.VMEM((2, width, pair), jnp.int32),
            pltpu.VMEM((nt, rows3, lanes), b16),
            pltpu.VMEM((nt, rows3 // 2, 128), b16),
            pltpu.VMEM((nt, rows3 // 2, 128), b16),
            pltpu.VMEM((nt, 16, rows3), b16),
            pltpu.VMEM((2, 16, rows3), b16),
            pltpu.VMEM((2, 16, rows3), b16),
            pltpu.VMEM((3, rows3, lanes), b16),
            pltpu.VMEM((3, 16, rows3), b16),
            pltpu.VMEM((nt, rows3 // 2, 256), b16),
            pltpu.VMEM((3, rows3 // 2, 256), b16),
            pltpu.VMEM((2, rows3, 128), b16),
            pltpu.VMEM((nt, width, 5 * lanes), b16),
            pltpu.VMEM((nt, width, 5 * lanes), b16),
            pltpu.VMEM((plane, width // 2, pair), f32),
            pltpu.VMEM((nt, width, pair), f32),
            pltpu.VMEM((OWNERS, 8, pair), f32),
            pltpu.VMEM((nt * plane, 8, pair), f32),
            pltpu.VMEM((OWNERS, 8, pair), f32),
            dma((3,)),
            dma((2, 3)),
            dma((2, 3)),
            dma((2, 2)),
            dma((2, 4)),
            dma((2, 4)),
            dma((plane,)),
            dma((1,)),
            dma((3,)),
            dma((1,)),
            dma((OWNERS,)),
            dma((1,)),
            dma((nt * plane,)),
            dma((2,)),
        ],
        compiler_params=pltpu.CompilerParams(
            collective_id=0, has_side_effects=True, vmem_limit_bytes=40 * 2**20
        ),
        name="gather",
    )(*(pltpu.with_memory_space_constraint(a, pltpu.HBM) for a in (velocity, seeds_first, seeds_merge.transpose(0, 2, 1))))
    strips = 5 * cells_x
    out = pl.pallas_call(
        tail_kernel,
        out_shape=jax.ShapeDtypeStruct((width * strips, quarter), f32),
        in_specs=[vmem] * 3,
        out_specs=hbm,
        scratch_shapes=[pltpu.VMEM((width * strips, quarter), f32), dma],
        compiler_params=pltpu.CompilerParams(vmem_limit_bytes=32 * 2**20),
        name="tail",
    )(weights, coarse, fine)
    return out.reshape(width, 5, cells_x, quarter)


def solution(mesh):
    in_specs = (P(None, "ta", "sx", "sy"), P(), P())
    out_specs = P(None, None, "sx", ("sy", "ta"))
    return jax.shard_map(local, mesh=mesh, in_specs=in_specs, out_specs=out_specs, check_vma=False)
```

```python
import functools

import jax
import jax.numpy as jnp
from jax import lax
from jax.experimental import pallas as pl
from jax.experimental.pallas import tpu as pltpu
from jax.sharding import PartitionSpec as P

HI = lax.Precision.HIGHEST
MESH = pl.DeviceIdType.MESH
OWNERS = 24
LEAD = 8


def mm(left, right, contract=(1, 0)):
    return lax.dot_general(
        left,
        right,
        (((contract[0],), (contract[1],)), ((), ())),
        precision=HI,
        preferred_element_type=jnp.float32,
    )


def dot16(left, right, contract=(1, 0)):
    return lax.dot_general(
        left,
        right,
        (((contract[0],), (contract[1],)), ((), ())),
        preferred_element_type=jnp.float32,
    )


def iotas(rows, cols):
    return (
        lax.broadcasted_iota(jnp.int32, (rows, cols), 0),
        lax.broadcasted_iota(jnp.int32, (rows, cols), 1),
    )


def eye(rows, cols):
    row, col = iotas(rows, cols)
    return (row == col).astype(jnp.float32)


def signed_half(plus, minus):
    return (0.5 * plus.astype(jnp.float32) - 0.5 * minus.astype(jnp.float32)).astype(jnp.bfloat16)


def tree(terms):
    while len(terms) > 1:
        terms = [a + b for a, b in zip(terms[::2], terms[1::2])]
    return terms[0]


def eliminate(mats, sides):
    n = mats[0].shape[0]
    tiles, width, single = n // 8, 2 * n, len(mats) == 1
    halves = [mats + sides] if single else [mats, sides]
    work = [[jnp.concatenate(h, axis=1)[8 * i : 8 * i + 8] for i in range(tiles)] for h in halves]
    sub = lax.broadcasted_iota(jnp.int32, (8, width), 0)
    left = lax.broadcasted_iota(jnp.int32, (8, width), 1) < n

    def spread(tile, row):
        return jnp.broadcast_to(tile[row : row + 1], (8, width))

    def column(i, j):
        tile = work[0][i]
        value = jnp.broadcast_to(tile[:, j : j + 1], (8, width))
        if single:
            return value
        return jnp.where(left, value, jnp.broadcast_to(tile[:, n + j : n + j + 1], (8, width)))

    done = [[None] * tiles for _ in work]
    now = [column(0, k) for k in range(8)]
    for p in range(tiles):
        more = p + 1 < tiles
        if more:
            below = [column(p + 1, 8 * p + k) for k in range(8)]
            head = [column(p, 8 * p + 8 + k) for k in range(8)]
            foot = [column(p + 1, 8 * p + 8 + k) for k in range(8)]
        raw = [[column(i, 8 * p + k) for k in range(8)] for i in range(p + 2, tiles)]
        scales = None
        for k in range(8):
            pivot = spread(now[k], k)
            inv = 1.0 / pivot
            root = lax.rsqrt(pivot)
            rows = [spread(w[p], k) for w in work]
            for d, row in zip(done, rows):
                d[p] = row * root if k == 0 else jnp.where(sub >= k, row * root, d[p])
            scales = inv if k == 0 else jnp.where(sub >= k, inv, scales)
            across = [spread(now[j], k) for j in range(k + 1, 8)]
            f = jnp.where(sub == k, 0.0, now[k]) * inv
            for w, row in zip(work, rows):
                w[p] = w[p] - f * row
            for j in range(k + 1, 8):
                now[j] = now[j] - f * across[j - k - 1]
            if more:
                ahead = [spread(h, k) for h in head]
                g = below[k] * inv
                for w, row in zip(work, rows):
                    w[p + 1] = w[p + 1] - g * row
                for j in range(k + 1, 8):
                    below[j] = below[j] - g * across[j - k - 1]
                for j in range(8):
                    foot[j] = foot[j] - g * ahead[j]
                    if k < 7:
                        head[j] = head[j] - f * ahead[j]
        for w in work:
            full = w[p] * scales
            spreads = [spread(full, k) for k in range(8)]
            for i in range(p + 2, tiles):
                w[i] = w[i] - tree([raw[i - p - 2][k] * spreads[k] for k in range(8)])
        if more:
            now = foot
    out = [jnp.concatenate(d, axis=0) for d in done]
    return [out[0][:, n:]] if single else [out[1][:, :n], out[1][:, n:]]


def total(entries):
    return jnp.sum(jnp.sum(entries, axis=0, keepdims=True), axis=1, keepdims=True)


def first_level(grams, first):
    width = first.shape[0]
    ident = eye(width, width)
    images = [mm(first, g, (0, 0)) for g in grams]
    reduced = [mm(z, first) for z in images]
    solved = eliminate(reduced, images)
    return [c * lax.rsqrt(total(g * ident) / width) for c, g in zip(solved, grams)]


def prepare(coefs, turn):
    width = turn.shape[0]
    lean = [mm(c, turn[:, i * width : (i + 1) * width], (0, 1)) for i, c in enumerate(coefs)]
    return jnp.concatenate(lean, axis=0), [mm(c, c, (0, 0)) for c in coefs]


def middle_level(pairs, ready):
    width = pairs[0].shape[0] // 2
    reduced, sides, scales = [], [], []
    for gram, (lean, norms) in zip(pairs, ready):
        image = mm(lean, gram, (0, 0))
        reduced.append(mm(image, lean))
        sides.append(
            jnp.concatenate([mm(image[:, :width], norms[0]), mm(image[:, width:], norms[1])], axis=1)
        )
        trace = total(norms[0] * gram[:width, :width]) + total(norms[1] * gram[width:, width:])
        scales.append(lax.rsqrt(trace / (2 * width)))
    inverses = eliminate(reduced, [eye(width, width)] * len(pairs))
    return [mm(inv, s) * k for inv, s, k in zip(inverses, sides, scales)]


def last_level(pairs, cross, weights, turn):
    width = turn.shape[0]
    lean = [mm(weights[u], turn[:, u * width : (u + 1) * width], (0, 1)) for u in (0, 1)]
    image = [mm(lean[u], pairs[u], (0, 0)) for u in (0, 1)]
    norms = [mm(weights[u], weights[u], (0, 0)) for u in (0, 1)]
    up = mm(lean[1], cross, (0, 0))
    down = mm(lean[0], cross, (0, 1))
    mixed = mm(up, lean[0])
    reduced = mm(image[0], lean[0]) + mm(image[1], lean[1]) + (mixed + mixed.T)
    trace = total(norms[0] * pairs[0]) + total(norms[1] * pairs[1])
    sides = jnp.concatenate([mm(image[0] + up, norms[0]), mm(image[1] + down, norms[1])], axis=1)
    inverse = eliminate([reduced], [eye(width, width)])[0]
    return mm(inverse, sides) * lax.rsqrt(trace / (2 * width))


def gather_kernel(
    quarter, nx, ny, nt,
    velocity_hbm, first_hbm, merge_hbm,
    coarse_ref, fine_ref, weight_ref,
    velocity, seeds_first, seeds_merge, chunk, edge_low, edge_high, column, rim_out,
    rims, land, column_in, halo_own, halo, passed,
    own_coarse, own_fine, own_landed, shared, parts, landed, whole,
    load_sems, chunk_sems, column_sems, rim_sems, low_sems, high_sems,
    own_sems, own_in, share_sems, share_in, scatter_sems, scatter_in, spread_sems, spread_in,
):
    ix, iy, it = lax.axis_index("sx"), lax.axis_index("sy"), lax.axis_index("ta")
    plane = nx * ny
    devices = plane * nt
    place = ix * ny + iy
    me = it * plane + place
    rows3, lanes = chunk.shape[1:]
    snaps = rows3 // 3
    cells_x = lanes // quarter
    half3 = rows3 // 2
    partner = it + 1 - 2 * lax.rem(it, 2)
    near, far = lax.rem(it + 2, 4), 3 - it
    b16, f32 = jnp.bfloat16, jnp.float32

    def device(t):
        where = lax.rem(t, plane)
        return (lax.div(where, ny), lax.rem(where, ny), lax.div(t, plane))

    def copy(src, dst, send, recv, target):
        return pltpu.make_async_remote_copy(
            src_ref=src, dst_ref=dst, send_sem=send, recv_sem=recv, device_id=target, device_id_type=MESH
        )

    loads = [
        pltpu.make_async_copy(src, dst, load_sems.at[i])
        for i, (src, dst) in enumerate(
            ((velocity_hbm, velocity), (first_hbm, seeds_first), (merge_hbm, seeds_merge))
        )
    ]
    for c in loads:
        c.start()

    barrier = pltpu.get_barrier_semaphore()

    def greet(target):
        pl.semaphore_signal(barrier, inc=1, device_id=target, device_id_type=MESH)

    def greet_plane(j, carry):
        t = lax.rem(place + j, plane)
        greet((lax.div(t, ny), lax.rem(t, ny), it))
        return carry

    others = (partner, near, far)
    for t in others:
        greet((ix, iy, t))
    can_up, can_down = ix < nx - 1, ix > 0
    lax.fori_loop(1, plane, greet_plane, 0)
    expected = plane - 1 + 3

    right_ok, left_ok = iy + 1 < ny, iy > 0

    @pl.when(jnp.logical_not(can_down))
    def _():
        halo[:, :, :128] = jnp.zeros((3, half3, 128), b16)
        halo_own[:, :, :128] = jnp.zeros((nt, half3, 128), b16)
        passed[0] = jnp.zeros((rows3, 128), b16)

    @pl.when(jnp.logical_not(can_up))
    def _():
        halo[:, :, 128:] = jnp.zeros((3, half3, 128), b16)
        halo_own[:, :, 128:] = jnp.zeros((nt, half3, 128), b16)
        passed[1] = jnp.zeros((rows3, 128), b16)

    @pl.when(jnp.logical_not(left_ok))
    def _():
        rims[0] = jnp.zeros((16, rows3), b16)

    @pl.when(jnp.logical_not(right_ok))
    def _():
        rims[1] = jnp.zeros((16, rows3), b16)

    row, lane = iotas(16, lanes)
    pick_right = ((row < cells_x) & (lane == row * quarter + quarter - 1)).astype(f32).astype(b16)
    pick_left = (
        ((row >= cells_x) & (row < 2 * cells_x) & (lane == (row - cells_x) * quarter))
        .astype(f32)
        .astype(b16)
    )

    loads[0].wait()
    for c in range(3):
        field = velocity[c].astype(f32)
        rows = [field[:, x, :] for x in range(cells_x)]
        for q in range(nt):
            cut = slice(q * quarter, (q + 1) * quarter)
            piece = jnp.concatenate([r[:, cut] for r in rows], axis=1)
            chunk[q, c * snaps : (c + 1) * snaps] = piece.astype(b16)
    for q in range(nt):
        whole_piece = chunk[q].astype(f32)
        first_row = whole_piece[:, :quarter]
        last_row = whole_piece[:, lanes - quarter :]
        edge_low[q] = jnp.concatenate([first_row[:half3], first_row[half3:]], axis=1).astype(b16)
        edge_high[q] = jnp.concatenate([last_row[:half3], last_row[half3:]], axis=1).astype(b16)
    right_of = [dot16(pick_right, chunk[q], (1, 1)) for q in range(nt)]
    left_of = [dot16(pick_left, chunk[q], (1, 1)) for q in range(nt)]
    rim_out[0] = right_of[nt - 1].astype(b16)
    rim_out[1] = left_of[0].astype(b16)
    for q in (1, 2):
        column[q] = (right_of[q - 1] + left_of[q + 1]).astype(b16)

    pl.semaphore_wait(barrier, expected)

    def chunk_copy(i):
        t = others[i]
        return copy(chunk.at[t], land.at[i], chunk_sems.at[0, i], chunk_sems.at[1, i], (ix, iy, t))

    def column_copy(i):
        t = others[i]
        return copy(column.at[t], column_in.at[i], column_sems.at[0, i], column_sems.at[1, i], (ix, iy, t))

    def edge_copy(source, side, sems, to_x, i):
        at = pl.ds(128 * side, 128)
        if i == 1:
            src = land.at[1, :, pl.ds((1 - side) * (lanes - 128), 128)]
            return copy(src, passed.at[side], sems.at[0, i], sems.at[1, i], (to_x, iy, it))
        if i < 3:
            t = others[i]
            return copy(halo_own.at[t, :, at], halo.at[i, :, at], sems.at[0, i], sems.at[1, i], (ix, iy, t))
        return copy(source, halo_own.at[:, :, at], sems.at[0, i], sems.at[1, i], (to_x, iy, it))

    def rim_copies():
        return (
            (right_ok, copy(rim_out.at[0], rims.at[0], rim_sems.at[0, 0], rim_sems.at[1, 0], (ix, jnp.minimum(iy + 1, ny - 1), it))),
            (left_ok, copy(rim_out.at[1], rims.at[1], rim_sems.at[0, 1], rim_sems.at[1, 1], (ix, jnp.maximum(iy - 1, 0), it))),
        )

    def high(i):
        return edge_copy(edge_high, 0, high_sems, jnp.minimum(ix + 1, nx - 1), i)

    def low(i):
        return edge_copy(edge_low, 1, low_sems, jnp.maximum(ix - 1, 0), i)

    def edges(i, act):
        if i in (1, 3):
            pl.when(can_up)(lambda: act(high(i)))
            pl.when(can_down)(lambda: act(low(i)))
        else:
            pl.when(can_down)(lambda: act(high(i)))
            pl.when(can_up)(lambda: act(low(i)))

    def start(c):
        c.start()

    for ok, c in rim_copies():
        pl.when(ok)(functools.partial(start, c))
    chunk_copy(1).start()
    edges(3, start)
    chunk_copy(0).start()
    chunk_copy(2).start()
    def halo_wait(i):
        pl.when(can_down)(lambda: high(i).wait_recv())
        pl.when(can_up)(lambda: low(i).wait_recv())

    pl.when(left_ok)(lambda: rim_copies()[0][1].wait_recv())
    pl.when(right_ok)(lambda: rim_copies()[1][1].wait_recv())
    column[0] = (rims[0].astype(f32) + left_of[1]).astype(b16)
    column[nt - 1] = (right_of[nt - 2] + rims[1].astype(f32)).astype(b16)
    for i in (2, 1, 0):
        column_copy(i).start()
    halo_wait(3)
    for i in (2, 0):
        edges(i, start)

    row, lane = iotas(lanes, lanes)
    gap = row - lane
    same = row // quarter == lane // quarter
    both = jnp.concatenate(
        [
            signed_half(gap == quarter, gap == -quarter),
            signed_half((gap == 1) & same, (gap == -1) & same),
        ],
        axis=1,
    )
    row, lane = iotas(256, 2 * lanes)
    wide, at = lane // lanes, lax.rem(lane, lanes)
    rise, k = row // 128, lax.rem(row, 128)
    hit = k // quarter == wide
    k = lax.rem(k, quarter)
    outer = signed_half(
        hit & (rise == 1) & (at == k + lanes - quarter), hit & (rise == 0) & (at == k)
    )
    row, lane = iotas(16, lanes)
    rim = signed_half(
        (row >= cells_x) & (row < 2 * cells_x) & (lane == (row - cells_x) * quarter + quarter - 1),
        (row < cells_x) & (lane == row * quarter),
    )

    row, lane = iotas(256, lanes)
    k = lax.rem(row, 128)
    beside = signed_half(
        (row >= 128) & (k < quarter) & (lane == k + lanes - quarter),
        (row < 128) & (lane == k - (128 - quarter)),
    )

    def strain(block, border, sides):
        inner = dot16(block, both)
        if border is None:
            across = dot16(jnp.concatenate([passed[0], passed[1]], axis=1), beside)
        else:
            across = dot16(border, outer)
            across = jnp.concatenate([across[:, :lanes], across[:, lanes:]], axis=0)
        dx = inner[:, :lanes] + across
        dy = inner[:, lanes:] + dot16(sides, rim, (0, 0))
        ux, vx, wx = (dx[i * snaps : (i + 1) * snaps] for i in range(3))
        uy, vy, wy = (dy[i * snaps : (i + 1) * snaps] for i in range(3))
        fields = jnp.concatenate([ux, vy, 0.5 * (uy + vx), 0.5 * wx, 0.5 * wy], axis=1)
        coarse = fields.astype(b16)
        return coarse, (fields - coarse.astype(f32)).astype(b16)

    def keep(block, values):
        at = pl.ds(pl.multiple_of(block * snaps, snaps), snaps)
        coarse_ref[at], fine_ref[at] = values

    own = jnp.zeros((snaps, 2 * snaps), f32)
    for q in range(nt):
        coarse, fine = strain(chunk[q], halo_own[q], column[q])
        own_coarse[q], own_fine[q] = coarse, fine
        own = own + dot16(coarse, jnp.concatenate([coarse, fine], axis=0), (1, 1))
    skew = own[:, snaps:]
    own = own[:, :snaps] + (skew + skew.T)
    half = snaps // 2
    own_landed[place] = jnp.concatenate([own[:half], own[half:]], axis=1)

    def own_copies(act):
        def body(j, carry):
            t = lax.rem(place + j, plane)
            act(
                copy(
                    own_landed.at[place], own_landed.at[place], own_sems.at[j], own_in.at[0],
                    (lax.div(t, ny), lax.rem(t, ny), it),
                )
            )
            return carry

        lax.fori_loop(1, plane, body, 0)

    own_copies(start)
    keep(it, (own_coarse[it], own_fine[it]))
    chunk_copy(1).wait_recv()
    edges(1, start)
    for i in (0, 2, 1):
        if i != 1:
            chunk_copy(i).wait_recv()
        halo_wait(i)
        column_copy(i).wait_recv()
        keep(others[i], strain(land[i], None if i == 1 else halo[i], column_in[i]))
    pair = 2 * snaps

    def gram(high, low):
        coarse, fine = coarse_ref[low], fine_ref[low]
        size = coarse.shape[0]
        both_low = dot16(coarse_ref[high], jnp.concatenate([coarse, fine], axis=0), (1, 1))
        return both_low[:, :size] + (both_low[:, size:] + dot16(fine_ref[high], coarse, (1, 1)))

    rank = jnp.where(it == 0, 2, jnp.where(it == 3, 3, it - 1)) * plane + place
    owner = rank < OWNERS
    slot = jnp.minimum(rank, OWNERS - 1)

    def scatter(first_piece, last_piece, act):
        for j in range(first_piece, last_piece):
            if j < LEAD:
                k = lax.rem(place + j, LEAD)
            else:
                k = LEAD + lax.rem(place + j, OWNERS - LEAD)
            group, where = lax.div(k, plane), lax.rem(k, plane)
            level = jnp.where(group == 2, 0, jnp.where(group == 3, 3, group + 1))
            c = copy(
                parts.at[k], landed.at[rank], scatter_sems.at[j], scatter_in.at[0],
                (lax.div(where, ny), lax.rem(where, ny), level),
            )
            pl.when(rank != k)(functools.partial(act, c))

    lead = slot < LEAD

    def spread(act):
        def body(t, carry):
            c = copy(
                whole.at[slot], whole.at[slot], spread_sems.at[t], spread_in.at[jnp.where(lead, 0, 1)],
                device(t),
            )
            pl.when(t != me)(functools.partial(act, c))
            return carry

        @pl.when(owner)
        def _():
            lax.fori_loop(0, devices, body, 0)

    blocks = [slice(b * snaps, (b + 1) * snaps) for b in range(nt)]
    mixed = jnp.concatenate([gram(blocks[1], blocks[0]), gram(blocks[3], blocks[2])], axis=1)
    parts[:LEAD] = mixed.reshape(LEAD, 8, pair)
    scatter(0, LEAD, start)
    parts[LEAD:] = gram(slice(pair, 2 * pair), slice(0, pair)).reshape(OWNERS - LEAD, 8, pair)
    scatter(LEAD, OWNERS, start)

    for c in loads[1:]:
        c.wait()
    first = eye(snaps, snaps) + seeds_first[...].astype(f32) * (0.5 / 512.0)
    stacked = jnp.concatenate([eye(snaps, snaps)] * 2, axis=1) * (2.0**-0.5)
    turns = [
        stacked + seeds_merge[level].astype(f32) * (0.5 / (64.0 * 128.0**0.5)) for level in range(2)
    ]
    some = own_landed.at[pl.ds(0, plane - 1)]
    copy(some, some, own_sems.at[0], own_in.at[0], (ix, iy, partner)).wait_recv()
    packed = jnp.sum(own_landed[...], axis=0)
    own = jnp.concatenate([packed[:, :snaps], packed[:, snaps:]], axis=0)
    shared[it] = jnp.concatenate([first_level([own], first)[0], own], axis=1)

    def share_copy(i):
        return copy(shared.at[it], shared.at[it], share_sems.at[i], share_in.at[0], (ix, iy, others[i]))

    for i in range(3):
        share_copy(i).start()

    @pl.when(owner)
    def _():
        landed[rank] = parts[slot]
        some = landed.at[pl.ds(0, devices - 1)]
        copy(some, some, scatter_sems.at[0], scatter_in.at[0], (ix, iy, partner)).wait_recv()
        whole[slot] = jnp.sum(landed[...], axis=0)

    spread(start)
    some = shared.at[pl.ds(0, nt - 1)]
    copy(some, some, share_sems.at[0], share_in.at[0], (ix, iy, partner)).wait_recv()
    coefs = [shared[b][:, :snaps] for b in range(nt)]
    grams = [shared[b][:, snaps:] for b in range(nt)]

    ready = [prepare(coefs[2 * u : 2 * u + 2], turns[0]) for u in range(2)]

    def arrived(part, first_piece, count, own_piece):
        def wait(pieces):
            some = whole.at[pl.ds(first_piece, pieces)]
            copy(some, some, spread_sems.at[0], spread_in.at[part], (ix, iy, partner)).wait_recv()

        pl.when(own_piece)(lambda: wait(count - 1))
        pl.when(jnp.logical_not(own_piece))(lambda: wait(count))
        return whole[first_piece : first_piece + count].reshape(count * 8, pair)

    def finish(c):
        c.wait_send()

    for ok, c in rim_copies():
        pl.when(ok)(functools.partial(finish, c))
    for i in range(3):
        finish(chunk_copy(i))
        finish(column_copy(i))
        finish(share_copy(i))
    for i in range(4):
        edges(i, finish)
    own_copies(finish)
    scatter(0, OWNERS, finish)
    spread(finish)

    rows = arrived(0, 0, LEAD, jnp.logical_and(owner, lead))
    pairs = []
    for u in range(2):
        mixed = rows[:, u * snaps : (u + 1) * snaps]
        pairs.append(
            jnp.concatenate(
                [
                    jnp.concatenate([grams[2 * u], mixed.T], axis=1),
                    jnp.concatenate([mixed, grams[2 * u + 1]], axis=1),
                ],
                axis=0,
            )
        )
    weights = middle_level(pairs, ready)
    cross = arrived(1, LEAD, OWNERS - LEAD, jnp.logical_and(owner, jnp.logical_not(lead)))
    weight_ref[...] = last_level(pairs, cross, weights, turns[1])


def tail_kernel(weight_ref, coarse_ref, fine_ref, out_hbm, out, sem):
    modes, lanes = weight_ref.shape[0], coarse_ref.shape[1]
    weights = weight_ref[...]
    coarse = weights.astype(jnp.bfloat16)
    fine = (weights - coarse.astype(jnp.float32)).astype(jnp.bfloat16)
    both = dot16(jnp.concatenate([coarse, fine], axis=0), coarse_ref[...])
    basis = both[:modes] + (both[modes:] + dot16(coarse, fine_ref[...]))
    quarter = out.shape[1]
    strips = lanes // quarter
    for i in range(strips):
        out[pl.ds(i, modes, stride=strips), :] = basis[:, i * quarter : (i + 1) * quarter]
    done = pltpu.make_async_copy(out, out_hbm, sem)
    done.start()
    done.wait()


def local(velocity, seeds_first, seeds_merge):
    comps, width, cells_x, cells_y = velocity.shape
    nx, ny, nt = (lax.axis_size(a) for a in ("sx", "sy", "ta"))
    quarter = cells_y // nt
    lanes = cells_x * quarter
    plane = nx * ny
    rows3 = comps * width
    pair = 2 * width
    vmem = pl.BlockSpec(memory_space=pltpu.VMEM)
    hbm = pl.BlockSpec(memory_space=pltpu.HBM)
    b16, f32 = jnp.bfloat16, jnp.float32
    dma = pltpu.SemaphoreType.DMA
    coarse, fine, weights = pl.pallas_call(
        functools.partial(gather_kernel, quarter, nx, ny, nt),
        out_shape=(
            jax.ShapeDtypeStruct((nt * width, 5 * lanes), b16),
            jax.ShapeDtypeStruct((nt * width, 5 * lanes), b16),
            jax.ShapeDtypeStruct((width, nt * width), f32),
        ),
        in_specs=[hbm] * 3,
        out_specs=(vmem,) * 3,
        scratch_shapes=[
            pltpu.VMEM(velocity.shape, b16),
            pltpu.VMEM((width, width), jnp.int32),
            pltpu.VMEM((2, width, pair), jnp.int32),
            pltpu.VMEM((nt, rows3, lanes), b16),
            pltpu.VMEM((nt, rows3 // 2, 128), b16),
            pltpu.VMEM((nt, rows3 // 2, 128), b16),
            pltpu.VMEM((nt, 16, rows3), b16),
            pltpu.VMEM((2, 16, rows3), b16),
            pltpu.VMEM((2, 16, rows3), b16),
            pltpu.VMEM((3, rows3, lanes), b16),
            pltpu.VMEM((3, 16, rows3), b16),
            pltpu.VMEM((nt, rows3 // 2, 256), b16),
            pltpu.VMEM((3, rows3 // 2, 256), b16),
            pltpu.VMEM((2, rows3, 128), b16),
            pltpu.VMEM((nt, width, 5 * lanes), b16),
            pltpu.VMEM((nt, width, 5 * lanes), b16),
            pltpu.VMEM((plane, width // 2, pair), f32),
            pltpu.VMEM((nt, width, pair), f32),
            pltpu.VMEM((OWNERS, 8, pair), f32),
            pltpu.VMEM((nt * plane, 8, pair), f32),
            pltpu.VMEM((OWNERS, 8, pair), f32),
            dma((3,)),
            dma((2, 3)),
            dma((2, 3)),
            dma((2, 2)),
            dma((2, 4)),
            dma((2, 4)),
            dma((plane,)),
            dma((1,)),
            dma((3,)),
            dma((1,)),
            dma((OWNERS,)),
            dma((1,)),
            dma((nt * plane,)),
            dma((2,)),
        ],
        compiler_params=pltpu.CompilerParams(
            collective_id=0, has_side_effects=True, vmem_limit_bytes=40 * 2**20
        ),
        name="gather",
    )(*(pltpu.with_memory_space_constraint(a, pltpu.HBM) for a in (velocity, seeds_first, seeds_merge.transpose(0, 2, 1))))
    strips = 5 * cells_x
    out = pl.pallas_call(
        tail_kernel,
        out_shape=jax.ShapeDtypeStruct((width * strips, quarter), f32),
        in_specs=[vmem] * 3,
        out_specs=hbm,
        scratch_shapes=[pltpu.VMEM((width * strips, quarter), f32), dma],
        compiler_params=pltpu.CompilerParams(vmem_limit_bytes=32 * 2**20),
        name="tail",
    )(weights, coarse, fine)
    return out.reshape(width, 5, cells_x, quarter)


def solution(mesh):
    in_specs = (P(None, "ta", "sx", "sy"), P(), P())
    out_specs = P(None, None, "sx", ("sy", "ta"))
    return jax.shard_map(local, mesh=mesh, in_specs=in_specs, out_specs=out_specs, check_vma=False)
```

```python
import functools

import jax
import jax.numpy as jnp
from jax import lax
from jax.experimental import pallas as pl
from jax.experimental.pallas import tpu as pltpu
from jax.sharding import PartitionSpec as P

HI = lax.Precision.HIGHEST
MESH = pl.DeviceIdType.MESH
OWNERS = 24
LEAD = 8


def mm(left, right, contract=(1, 0)):
    return lax.dot_general(
        left,
        right,
        (((contract[0],), (contract[1],)), ((), ())),
        precision=HI,
        preferred_element_type=jnp.float32,
    )


def dot16(left, right, contract=(1, 0)):
    return lax.dot_general(
        left,
        right,
        (((contract[0],), (contract[1],)), ((), ())),
        preferred_element_type=jnp.float32,
    )


def iotas(rows, cols):
    return (
        lax.broadcasted_iota(jnp.int32, (rows, cols), 0),
        lax.broadcasted_iota(jnp.int32, (rows, cols), 1),
    )


def eye(rows, cols):
    row, col = iotas(rows, cols)
    return (row == col).astype(jnp.float32)


def signed_half(plus, minus):
    return (0.5 * plus.astype(jnp.float32) - 0.5 * minus.astype(jnp.float32)).astype(jnp.bfloat16)


def tree(terms):
    while len(terms) > 1:
        terms = [a + b for a, b in zip(terms[::2], terms[1::2])]
    return terms[0]


def eliminate(mats, sides):
    n = mats[0].shape[0]
    tiles, width, single = n // 8, 2 * n, len(mats) == 1
    halves = [mats + sides] if single else [mats, sides]
    work = [[jnp.concatenate(h, axis=1)[8 * i : 8 * i + 8] for i in range(tiles)] for h in halves]
    sub = lax.broadcasted_iota(jnp.int32, (8, width), 0)
    left = lax.broadcasted_iota(jnp.int32, (8, width), 1) < n

    def spread(tile, row):
        return jnp.broadcast_to(tile[row : row + 1], (8, width))

    def column(i, j):
        tile = work[0][i]
        value = jnp.broadcast_to(tile[:, j : j + 1], (8, width))
        if single:
            return value
        return jnp.where(left, value, jnp.broadcast_to(tile[:, n + j : n + j + 1], (8, width)))

    done = [[None] * tiles for _ in work]
    now = [column(0, k) for k in range(8)]
    for p in range(tiles):
        more = p + 1 < tiles
        if more:
            below = [column(p + 1, 8 * p + k) for k in range(8)]
            head = [column(p, 8 * p + 8 + k) for k in range(8)]
            foot = [column(p + 1, 8 * p + 8 + k) for k in range(8)]
        raw = [[column(i, 8 * p + k) for k in range(8)] for i in range(p + 2, tiles)]
        scales = None
        for k in range(8):
            pivot = spread(now[k], k)
            inv = 1.0 / pivot
            root = lax.rsqrt(pivot)
            rows = [spread(w[p], k) for w in work]
            for d, row in zip(done, rows):
                d[p] = row * root if k == 0 else jnp.where(sub >= k, row * root, d[p])
            scales = inv if k == 0 else jnp.where(sub >= k, inv, scales)
            across = [spread(now[j], k) for j in range(k + 1, 8)]
            f = jnp.where(sub == k, 0.0, now[k]) * inv
            for w, row in zip(work, rows):
                w[p] = w[p] - f * row
            for j in range(k + 1, 8):
                now[j] = now[j] - f * across[j - k - 1]
            if more:
                ahead = [spread(h, k) for h in head]
                g = below[k] * inv
                for w, row in zip(work, rows):
                    w[p + 1] = w[p + 1] - g * row
                for j in range(k + 1, 8):
                    below[j] = below[j] - g * across[j - k - 1]
                for j in range(8):
                    foot[j] = foot[j] - g * ahead[j]
                    if k < 7:
                        head[j] = head[j] - f * ahead[j]
        for w in work:
            full = w[p] * scales
            spreads = [spread(full, k) for k in range(8)]
            for i in range(p + 2, tiles):
                w[i] = w[i] - tree([raw[i - p - 2][k] * spreads[k] for k in range(8)])
        if more:
            now = foot
    out = [jnp.concatenate(d, axis=0) for d in done]
    return [out[0][:, n:]] if single else [out[1][:, :n], out[1][:, n:]]


def total(entries):
    return jnp.sum(jnp.sum(entries, axis=0, keepdims=True), axis=1, keepdims=True)


def first_level(grams, first):
    width = first.shape[0]
    ident = eye(width, width)
    images = [mm(first, g, (0, 0)) for g in grams]
    reduced = [mm(z, first) for z in images]
    solved = eliminate(reduced, images)
    return [c * lax.rsqrt(total(g * ident) / width) for c, g in zip(solved, grams)]


def prepare(coefs, turn):
    width = turn.shape[0]
    lean = [mm(c, turn[:, i * width : (i + 1) * width], (0, 1)) for i, c in enumerate(coefs)]
    return jnp.concatenate(lean, axis=0), [mm(c, c, (0, 0)) for c in coefs]


def middle_level(pairs, ready):
    width = pairs[0].shape[0] // 2
    reduced, sides, scales = [], [], []
    for gram, (lean, norms) in zip(pairs, ready):
        image = mm(lean, gram, (0, 0))
        reduced.append(mm(image, lean))
        sides.append(
            jnp.concatenate([mm(image[:, :width], norms[0]), mm(image[:, width:], norms[1])], axis=1)
        )
        trace = total(norms[0] * gram[:width, :width]) + total(norms[1] * gram[width:, width:])
        scales.append(lax.rsqrt(trace / (2 * width)))
    inverses = eliminate(reduced, [eye(width, width)] * len(pairs))
    return [mm(inv, s) * k for inv, s, k in zip(inverses, sides, scales)]


def last_level(pairs, cross, weights, turn):
    width = turn.shape[0]
    lean = [mm(weights[u], turn[:, u * width : (u + 1) * width], (0, 1)) for u in (0, 1)]
    image = [mm(lean[u], pairs[u], (0, 0)) for u in (0, 1)]
    norms = [mm(weights[u], weights[u], (0, 0)) for u in (0, 1)]
    up = mm(lean[1], cross, (0, 0))
    down = mm(lean[0], cross, (0, 1))
    mixed = mm(up, lean[0])
    reduced = mm(image[0], lean[0]) + mm(image[1], lean[1]) + (mixed + mixed.T)
    trace = total(norms[0] * pairs[0]) + total(norms[1] * pairs[1])
    sides = jnp.concatenate([mm(image[0] + up, norms[0]), mm(image[1] + down, norms[1])], axis=1)
    inverse = eliminate([reduced], [eye(width, width)])[0]
    return mm(inverse, sides) * lax.rsqrt(trace / (2 * width))


def gather_kernel(
    quarter, nx, ny, nt,
    velocity_hbm, first_hbm, merge_hbm,
    coarse_ref, fine_ref, weight_ref,
    velocity, seeds_first, seeds_merge, chunk, edge_low, edge_high, column, rim_out,
    rims, land, column_in, halo_own, halo, passed,
    own_coarse, own_fine, own_landed, shared, parts, landed, whole,
    load_sems, chunk_sems, column_sems, rim_sems, low_sems, high_sems,
    own_sems, own_in, share_sems, share_in, scatter_sems, scatter_in, spread_sems, spread_in,
):
    ix, iy, it = lax.axis_index("sx"), lax.axis_index("sy"), lax.axis_index("ta")
    plane = nx * ny
    devices = plane * nt
    place = ix * ny + iy
    me = it * plane + place
    rows3, lanes = chunk.shape[1:]
    snaps = rows3 // 3
    cells_x = lanes // quarter
    half3 = rows3 // 2
    partner = it + 1 - 2 * lax.rem(it, 2)
    near, far = lax.rem(it + 2, 4), 3 - it
    b16, f32 = jnp.bfloat16, jnp.float32

    def device(t):
        where = lax.rem(t, plane)
        return (lax.div(where, ny), lax.rem(where, ny), lax.div(t, plane))

    def copy(src, dst, send, recv, target):
        return pltpu.make_async_remote_copy(
            src_ref=src, dst_ref=dst, send_sem=send, recv_sem=recv, device_id=target, device_id_type=MESH
        )

    loads = [
        pltpu.make_async_copy(src, dst, load_sems.at[i])
        for i, (src, dst) in enumerate(
            ((velocity_hbm, velocity), (first_hbm, seeds_first), (merge_hbm, seeds_merge))
        )
    ]
    barrier = pltpu.get_barrier_semaphore()

    def greet(target):
        pl.semaphore_signal(barrier, inc=1, device_id=target, device_id_type=MESH)

    def greet_plane(j, carry):
        t = lax.rem(place + j, plane)
        greet((lax.div(t, ny), lax.rem(t, ny), it))
        return carry

    others = (partner, near, far)
    for t in others:
        greet((ix, iy, t))
    can_up, can_down = ix < nx - 1, ix > 0
    lax.fori_loop(1, plane, greet_plane, 0)
    for c in loads:
        c.start()
    expected = plane - 1 + 3

    right_ok, left_ok = iy + 1 < ny, iy > 0

    @pl.when(jnp.logical_not(can_down))
    def _():
        halo[:, :, :128] = jnp.zeros((3, half3, 128), b16)
        halo_own[:, :, :128] = jnp.zeros((nt, half3, 128), b16)
        passed[0] = jnp.zeros((rows3, 128), b16)

    @pl.when(jnp.logical_not(can_up))
    def _():
        halo[:, :, 128:] = jnp.zeros((3, half3, 128), b16)
        halo_own[:, :, 128:] = jnp.zeros((nt, half3, 128), b16)
        passed[1] = jnp.zeros((rows3, 128), b16)

    @pl.when(jnp.logical_not(left_ok))
    def _():
        rims[0] = jnp.zeros((16, rows3), b16)

    @pl.when(jnp.logical_not(right_ok))
    def _():
        rims[1] = jnp.zeros((16, rows3), b16)

    row, lane = iotas(16, lanes)
    pick_right = ((row < cells_x) & (lane == row * quarter + quarter - 1)).astype(f32).astype(b16)
    pick_left = (
        ((row >= cells_x) & (row < 2 * cells_x) & (lane == (row - cells_x) * quarter))
        .astype(f32)
        .astype(b16)
    )

    loads[0].wait()
    for c in range(3):
        field = velocity[c].astype(f32)
        rows = [field[:, x, :] for x in range(cells_x)]
        for q in range(nt):
            cut = slice(q * quarter, (q + 1) * quarter)
            piece = jnp.concatenate([r[:, cut] for r in rows], axis=1)
            chunk[q, c * snaps : (c + 1) * snaps] = piece.astype(b16)
    for q in range(nt):
        whole_piece = chunk[q].astype(f32)
        first_row = whole_piece[:, :quarter]
        last_row = whole_piece[:, lanes - quarter :]
        edge_low[q] = jnp.concatenate([first_row[:half3], first_row[half3:]], axis=1).astype(b16)
        edge_high[q] = jnp.concatenate([last_row[:half3], last_row[half3:]], axis=1).astype(b16)
    right_of = [dot16(pick_right, chunk[q], (1, 1)) for q in range(nt)]
    left_of = [dot16(pick_left, chunk[q], (1, 1)) for q in range(nt)]
    rim_out[0] = right_of[nt - 1].astype(b16)
    rim_out[1] = left_of[0].astype(b16)
    for q in (1, 2):
        column[q] = (right_of[q - 1] + left_of[q + 1]).astype(b16)

    pl.semaphore_wait(barrier, expected)

    def chunk_copy(i):
        t = others[i]
        return copy(chunk.at[t], land.at[i], chunk_sems.at[0, i], chunk_sems.at[1, i], (ix, iy, t))

    def column_copy(i):
        t = others[i]
        return copy(column.at[t], column_in.at[i], column_sems.at[0, i], column_sems.at[1, i], (ix, iy, t))

    def edge_copy(source, side, sems, to_x, i):
        at = pl.ds(128 * side, 128)
        if i == 1:
            src = land.at[1, :, pl.ds((1 - side) * (lanes - 128), 128)]
            return copy(src, passed.at[side], sems.at[0, i], sems.at[1, i], (to_x, iy, it))
        if i < 3:
            t = others[i]
            return copy(halo_own.at[t, :, at], halo.at[i, :, at], sems.at[0, i], sems.at[1, i], (ix, iy, t))
        return copy(source, halo_own.at[:, :, at], sems.at[0, i], sems.at[1, i], (to_x, iy, it))

    def rim_copies():
        return (
            (right_ok, copy(rim_out.at[0], rims.at[0], rim_sems.at[0, 0], rim_sems.at[1, 0], (ix, jnp.minimum(iy + 1, ny - 1), it))),
            (left_ok, copy(rim_out.at[1], rims.at[1], rim_sems.at[0, 1], rim_sems.at[1, 1], (ix, jnp.maximum(iy - 1, 0), it))),
        )

    def high(i):
        return edge_copy(edge_high, 0, high_sems, jnp.minimum(ix + 1, nx - 1), i)

    def low(i):
        return edge_copy(edge_low, 1, low_sems, jnp.maximum(ix - 1, 0), i)

    def edges(i, act):
        if i in (1, 3):
            pl.when(can_up)(lambda: act(high(i)))
            pl.when(can_down)(lambda: act(low(i)))
        else:
            pl.when(can_down)(lambda: act(high(i)))
            pl.when(can_up)(lambda: act(low(i)))

    def start(c):
        c.start()

    for ok, c in rim_copies():
        pl.when(ok)(functools.partial(start, c))
    chunk_copy(1).start()
    edges(3, start)
    chunk_copy(0).start()
    chunk_copy(2).start()
    def halo_wait(i):
        pl.when(can_down)(lambda: high(i).wait_recv())
        pl.when(can_up)(lambda: low(i).wait_recv())

    pl.when(left_ok)(lambda: rim_copies()[0][1].wait_recv())
    pl.when(right_ok)(lambda: rim_copies()[1][1].wait_recv())
    column[0] = (rims[0].astype(f32) + left_of[1]).astype(b16)
    column[nt - 1] = (right_of[nt - 2] + rims[1].astype(f32)).astype(b16)
    for i in (2, 1, 0):
        column_copy(i).start()
    halo_wait(3)
    for i in (2, 0):
        edges(i, start)

    row, lane = iotas(lanes, lanes)
    gap = row - lane
    same = row // quarter == lane // quarter
    both = jnp.concatenate(
        [
            signed_half(gap == quarter, gap == -quarter),
            signed_half((gap == 1) & same, (gap == -1) & same),
        ],
        axis=1,
    )
    row, lane = iotas(256, 2 * lanes)
    wide, at = lane // lanes, lax.rem(lane, lanes)
    rise, k = row // 128, lax.rem(row, 128)
    hit = k // quarter == wide
    k = lax.rem(k, quarter)
    outer = signed_half(
        hit & (rise == 1) & (at == k + lanes - quarter), hit & (rise == 0) & (at == k)
    )
    row, lane = iotas(16, lanes)
    rim = signed_half(
        (row >= cells_x) & (row < 2 * cells_x) & (lane == (row - cells_x) * quarter + quarter - 1),
        (row < cells_x) & (lane == row * quarter),
    )

    row, lane = iotas(256, lanes)
    k = lax.rem(row, 128)
    beside = signed_half(
        (row >= 128) & (k < quarter) & (lane == k + lanes - quarter),
        (row < 128) & (lane == k - (128 - quarter)),
    )

    def strain(block, border, sides):
        inner = dot16(block, both)
        if border is None:
            across = dot16(jnp.concatenate([passed[0], passed[1]], axis=1), beside)
        else:
            across = dot16(border, outer)
            across = jnp.concatenate([across[:, :lanes], across[:, lanes:]], axis=0)
        dx = inner[:, :lanes] + across
        dy = inner[:, lanes:] + dot16(sides, rim, (0, 0))
        ux, vx, wx = (dx[i * snaps : (i + 1) * snaps] for i in range(3))
        uy, vy, wy = (dy[i * snaps : (i + 1) * snaps] for i in range(3))
        fields = jnp.concatenate([ux, vy, 0.5 * (uy + vx), 0.5 * wx, 0.5 * wy], axis=1)
        coarse = fields.astype(b16)
        return coarse, (fields - coarse.astype(f32)).astype(b16)

    def keep(block, values):
        at = pl.ds(pl.multiple_of(block * snaps, snaps), snaps)
        coarse_ref[at], fine_ref[at] = values

    own = jnp.zeros((snaps, 2 * snaps), f32)
    for q in range(nt):
        coarse, fine = strain(chunk[q], halo_own[q], column[q])
        own_coarse[q], own_fine[q] = coarse, fine
        own = own + dot16(coarse, jnp.concatenate([coarse, fine], axis=0), (1, 1))
    skew = own[:, snaps:]
    own = own[:, :snaps] + (skew + skew.T)
    half = snaps // 2
    own_landed[place] = jnp.concatenate([own[:half], own[half:]], axis=1)

    def own_copies(act):
        def body(j, carry):
            t = lax.rem(place + j, plane)
            act(
                copy(
                    own_landed.at[place], own_landed.at[place], own_sems.at[j], own_in.at[0],
                    (lax.div(t, ny), lax.rem(t, ny), it),
                )
            )
            return carry

        lax.fori_loop(1, plane, body, 0)

    own_copies(start)
    keep(it, (own_coarse[it], own_fine[it]))
    chunk_copy(1).wait_recv()
    edges(1, start)
    for i in (0, 2, 1):
        if i != 1:
            chunk_copy(i).wait_recv()
        halo_wait(i)
        column_copy(i).wait_recv()
        keep(others[i], strain(land[i], None if i == 1 else halo[i], column_in[i]))
    pair = 2 * snaps

    def gram(high, low):
        coarse, fine = coarse_ref[low], fine_ref[low]
        size = coarse.shape[0]
        both_low = dot16(coarse_ref[high], jnp.concatenate([coarse, fine], axis=0), (1, 1))
        return both_low[:, :size] + (both_low[:, size:] + dot16(fine_ref[high], coarse, (1, 1)))

    rank = jnp.where(it == 0, 2, jnp.where(it == 3, 3, it - 1)) * plane + place
    owner = rank < OWNERS
    slot = jnp.minimum(rank, OWNERS - 1)

    def scatter(first_piece, last_piece, act):
        for j in range(first_piece, last_piece):
            if j < LEAD:
                k = lax.rem(place + j, LEAD)
            else:
                k = LEAD + lax.rem(place + j, OWNERS - LEAD)
            group, where = lax.div(k, plane), lax.rem(k, plane)
            level = jnp.where(group == 2, 0, jnp.where(group == 3, 3, group + 1))
            c = copy(
                parts.at[k], landed.at[rank], scatter_sems.at[j], scatter_in.at[0],
                (lax.div(where, ny), lax.rem(where, ny), level),
            )
            pl.when(rank != k)(functools.partial(act, c))

    lead = slot < LEAD

    def spread(act):
        def body(t, carry):
            c = copy(
                whole.at[slot], whole.at[slot], spread_sems.at[t], spread_in.at[jnp.where(lead, 0, 1)],
                device(t),
            )
            pl.when(t != me)(functools.partial(act, c))
            return carry

        @pl.when(owner)
        def _():
            lax.fori_loop(0, devices, body, 0)

    blocks = [slice(b * snaps, (b + 1) * snaps) for b in range(nt)]
    mixed = jnp.concatenate([gram(blocks[1], blocks[0]), gram(blocks[3], blocks[2])], axis=1)
    parts[:LEAD] = mixed.reshape(LEAD, 8, pair)
    scatter(0, LEAD, start)
    parts[LEAD:] = gram(slice(pair, 2 * pair), slice(0, pair)).reshape(OWNERS - LEAD, 8, pair)
    scatter(LEAD, OWNERS, start)

    for c in loads[1:]:
        c.wait()
    first = eye(snaps, snaps) + seeds_first[...].astype(f32) * (0.5 / 512.0)
    stacked = jnp.concatenate([eye(snaps, snaps)] * 2, axis=1) * (2.0**-0.5)
    turns = [
        stacked + seeds_merge[level].astype(f32) * (0.5 / (64.0 * 128.0**0.5)) for level in range(2)
    ]
    some = own_landed.at[pl.ds(0, plane - 1)]
    copy(some, some, own_sems.at[0], own_in.at[0], (ix, iy, partner)).wait_recv()
    packed = jnp.sum(own_landed[...], axis=0)
    own = jnp.concatenate([packed[:, :snaps], packed[:, snaps:]], axis=0)
    shared[it] = jnp.concatenate([first_level([own], first)[0], own], axis=1)

    def share_copy(i):
        return copy(shared.at[it], shared.at[it], share_sems.at[i], share_in.at[0], (ix, iy, others[i]))

    for i in range(3):
        share_copy(i).start()

    @pl.when(owner)
    def _():
        landed[rank] = parts[slot]
        some = landed.at[pl.ds(0, devices - 1)]
        copy(some, some, scatter_sems.at[0], scatter_in.at[0], (ix, iy, partner)).wait_recv()
        whole[slot] = jnp.sum(landed[...], axis=0)

    spread(start)
    some = shared.at[pl.ds(0, nt - 1)]
    copy(some, some, share_sems.at[0], share_in.at[0], (ix, iy, partner)).wait_recv()
    coefs = [shared[b][:, :snaps] for b in range(nt)]
    grams = [shared[b][:, snaps:] for b in range(nt)]

    ready = [prepare(coefs[2 * u : 2 * u + 2], turns[0]) for u in range(2)]

    def arrived(part, first_piece, count, own_piece):
        def wait(pieces):
            some = whole.at[pl.ds(first_piece, pieces)]
            copy(some, some, spread_sems.at[0], spread_in.at[part], (ix, iy, partner)).wait_recv()

        pl.when(own_piece)(lambda: wait(count - 1))
        pl.when(jnp.logical_not(own_piece))(lambda: wait(count))
        return whole[first_piece : first_piece + count].reshape(count * 8, pair)

    def finish(c):
        c.wait_send()

    for ok, c in rim_copies():
        pl.when(ok)(functools.partial(finish, c))
    for i in range(3):
        finish(chunk_copy(i))
        finish(column_copy(i))
        finish(share_copy(i))
    for i in range(4):
        edges(i, finish)
    own_copies(finish)
    scatter(0, OWNERS, finish)
    spread(finish)

    rows = arrived(0, 0, LEAD, jnp.logical_and(owner, lead))
    pairs = []
    for u in range(2):
        mixed = rows[:, u * snaps : (u + 1) * snaps]
        pairs.append(
            jnp.concatenate(
                [
                    jnp.concatenate([grams[2 * u], mixed.T], axis=1),
                    jnp.concatenate([mixed, grams[2 * u + 1]], axis=1),
                ],
                axis=0,
            )
        )
    weights = middle_level(pairs, ready)
    cross = arrived(1, LEAD, OWNERS - LEAD, jnp.logical_and(owner, jnp.logical_not(lead)))
    weight_ref[...] = last_level(pairs, cross, weights, turns[1])


def tail_kernel(weight_ref, coarse_ref, fine_ref, out_hbm, out, sem):
    modes, lanes = weight_ref.shape[0], coarse_ref.shape[1]
    weights = weight_ref[...]
    coarse = weights.astype(jnp.bfloat16)
    fine = (weights - coarse.astype(jnp.float32)).astype(jnp.bfloat16)
    both = dot16(jnp.concatenate([coarse, fine], axis=0), coarse_ref[...])
    basis = both[:modes] + (both[modes:] + dot16(coarse, fine_ref[...]))
    quarter = out.shape[1]
    strips = lanes // quarter
    for i in range(strips):
        out[pl.ds(i, modes, stride=strips), :] = basis[:, i * quarter : (i + 1) * quarter]
    done = pltpu.make_async_copy(out, out_hbm, sem)
    done.start()
    done.wait()


def local(velocity, seeds_first, seeds_merge):
    comps, width, cells_x, cells_y = velocity.shape
    nx, ny, nt = (lax.axis_size(a) for a in ("sx", "sy", "ta"))
    quarter = cells_y // nt
    lanes = cells_x * quarter
    plane = nx * ny
    rows3 = comps * width
    pair = 2 * width
    vmem = pl.BlockSpec(memory_space=pltpu.VMEM)
    hbm = pl.BlockSpec(memory_space=pltpu.HBM)
    b16, f32 = jnp.bfloat16, jnp.float32
    dma = pltpu.SemaphoreType.DMA
    coarse, fine, weights = pl.pallas_call(
        functools.partial(gather_kernel, quarter, nx, ny, nt),
        out_shape=(
            jax.ShapeDtypeStruct((nt * width, 5 * lanes), b16),
            jax.ShapeDtypeStruct((nt * width, 5 * lanes), b16),
            jax.ShapeDtypeStruct((width, nt * width), f32),
        ),
        in_specs=[hbm] * 3,
        out_specs=(vmem,) * 3,
        scratch_shapes=[
            pltpu.VMEM(velocity.shape, b16),
            pltpu.VMEM((width, width), jnp.int32),
            pltpu.VMEM((2, width, pair), jnp.int32),
            pltpu.VMEM((nt, rows3, lanes), b16),
            pltpu.VMEM((nt, rows3 // 2, 128), b16),
            pltpu.VMEM((nt, rows3 // 2, 128), b16),
            pltpu.VMEM((nt, 16, rows3), b16),
            pltpu.VMEM((2, 16, rows3), b16),
            pltpu.VMEM((2, 16, rows3), b16),
            pltpu.VMEM((3, rows3, lanes), b16),
            pltpu.VMEM((3, 16, rows3), b16),
            pltpu.VMEM((nt, rows3 // 2, 256), b16),
            pltpu.VMEM((3, rows3 // 2, 256), b16),
            pltpu.VMEM((2, rows3, 128), b16),
            pltpu.VMEM((nt, width, 5 * lanes), b16),
            pltpu.VMEM((nt, width, 5 * lanes), b16),
            pltpu.VMEM((plane, width // 2, pair), f32),
            pltpu.VMEM((nt, width, pair), f32),
            pltpu.VMEM((OWNERS, 8, pair), f32),
            pltpu.VMEM((nt * plane, 8, pair), f32),
            pltpu.VMEM((OWNERS, 8, pair), f32),
            dma((3,)),
            dma((2, 3)),
            dma((2, 3)),
            dma((2, 2)),
            dma((2, 4)),
            dma((2, 4)),
            dma((plane,)),
            dma((1,)),
            dma((3,)),
            dma((1,)),
            dma((OWNERS,)),
            dma((1,)),
            dma((nt * plane,)),
            dma((2,)),
        ],
        compiler_params=pltpu.CompilerParams(
            collective_id=0, has_side_effects=True, vmem_limit_bytes=40 * 2**20
        ),
        name="gather",
    )(*(pltpu.with_memory_space_constraint(a, pltpu.HBM) for a in (velocity, seeds_first, seeds_merge.transpose(0, 2, 1))))
    strips = 5 * cells_x
    out = pl.pallas_call(
        tail_kernel,
        out_shape=jax.ShapeDtypeStruct((width * strips, quarter), f32),
        in_specs=[vmem] * 3,
        out_specs=hbm,
        scratch_shapes=[pltpu.VMEM((width * strips, quarter), f32), dma],
        compiler_params=pltpu.CompilerParams(vmem_limit_bytes=32 * 2**20),
        name="tail",
    )(weights, coarse, fine)
    return out.reshape(width, 5, cells_x, quarter)


def solution(mesh):
    in_specs = (P(None, "ta", "sx", "sy"), P(), P())
    out_specs = P(None, None, "sx", ("sy", "ta"))
    return jax.shard_map(local, mesh=mesh, in_specs=in_specs, out_specs=out_specs, check_vma=False)
```
